128 devices in a mesh: section: 2 (over z_hi), fsdp: 4 (over x), dp: 16 (over z_lo, y, core).
Axes of the slice: x: 4, y: 4, z: 4 (z_hi: 2, z_lo: 2; z = z_hi * 2 + z_lo), core: 2. Of those that a mesh axis runs over, the one named last changes fastest.
Arguments:
- boundary: bfloat16 [2, 3, 1, 8192, 768], P('section', None, None, ('dp', 'fsdp')), may hold values from -6 to 6
- seq_ids: int32 [3, 1, 8192], P(None, None, 'dp'), may hold values from -1 to 1, as said below
- w_qkv: bfloat16 [2, 768, 2304], P('section', 'fsdp'), may hold values from -0.21875 to 0.21875
- w_out: bfloat16 [2, 768, 768], P('section', 'fsdp'), may hold values from -0.875 to 0.875
- w_in: bfloat16 [2, 768, 3072], P('section', 'fsdp'), may hold values from -0.21875 to 0.21875
- w_down: bfloat16 [2, 3072, 768], P('section', 'fsdp'), may hold values from -0.109375 to 0.109375
- gains: bfloat16 [2, 2, 768], P('section', None, 'fsdp'), may hold values from 0.5 to 1.5
- biases: bfloat16 [2, 6, 768], P('section', None, 'fsdp'), may hold values from -1.796875 to 1.796875
- b_in: bfloat16 [2, 3072], P('section', 'fsdp'), may hold values from -1.796875 to 1.796875
Outputs:
- boundary_out: float32 [2, 3, 1, 8192, 768], P('section', None, None, ('dp', 'fsdp'))
- g_qkv: float32 [2, 768, 2304], P('section', 'fsdp')
- g_out: float32 [2, 768, 768], P('section', 'fsdp')
- g_in: float32 [2, 768, 3072], P('section', 'fsdp')
- g_down: float32 [2, 3072, 768], P('section', 'fsdp')
- g_gains: float32 [2, 2, 768], P('section', None, 'fsdp')
- g_biases: float32 [2, 6, 768], P('section', None, 'fsdp')
- g_bin: float32 [2, 3072], P('section', 'fsdp')
The draws below stay inside these ranges and needn't reach their ends.
Inputs may be any that keep to these rules, and one draw needn't show every extreme that they name: `seq_ids`: in each slot of 512 tokens the numbers run 0 then 1 in contiguous runs (a run may be empty), then -1 to the slot's end; one of the two sequences in every slot is longer than 384 tokens, and some slot is one full sequence.
All inputs are finite; a program needn't handle non-finite values.
Results may differ from the reference program's by a relative error of at most 0.018.
Values may be sent and summed in bfloat16 or wider, within the bound.
No kernel may reach another device: no remote copies, remote signals or barrier semaphores. Data moves between devices by JAX's collectives and lax.ppermute only.
A program may use at most 192 MiB of HBM per device.

```python
import math
import jax
import jax.numpy as jnp
from jax import lax

HD = 64
FF = 3072
MODEL_WIDTH = 768
SLOT = 512
MICRO_BATCHES = 3
REPLICA_SLOTS = 1
SLOT_TOKENS = 8192
N_DP = 16


def draw_seq_ids(key, part):
    key = jax.random.fold_in(key, 7)
    replica_count = SLOT_TOKENS // SLOT
    total_slot_count = MICRO_BATCHES * REPLICA_SLOTS * replica_count
    key_list = jax.random.split(key, 4)
    floor_len = 3 * SLOT // 4 + 1
    long_len = jax.random.randint(key_list[0], (total_slot_count,), floor_len, SLOT + 1)
    chosen = jax.random.randint(key_list[1], (), 0, total_slot_count)
    second_pick = (chosen + 1) % total_slot_count
    slot_order = jnp.arange(total_slot_count)
    long_len = jnp.where(slot_order == chosen, SLOT, long_len)
    long_len = jnp.where(slot_order == second_pick, floor_len, long_len)
    room_left = SLOT - long_len
    short_len = jax.random.randint(key_list[2], (total_slot_count,), 0, room_left + 1)
    short_len = jnp.where(slot_order == second_pick, 1, short_len)
    long_first = jax.random.randint(key_list[3], (total_slot_count,), 0, 2)
    long_first = jnp.where(slot_order == second_pick, 0, long_first)
    first_len = jnp.where(long_first == 1, long_len, short_len)
    second_len = jnp.where(long_first == 1, short_len, long_len)
    position = jnp.arange(SLOT)[None, :]
    sequence_markers = jnp.where(position < first_len[:, None], 0, jnp.where(position < (first_len + second_len)[:, None], 1, -1))
    return sequence_markers.reshape(MICRO_BATCHES, REPLICA_SLOTS, SLOT_TOKENS).astype(jnp.int32)


def levels(rng, extent, cuts, smallest, high):
    factor_of = 1.0
    for axis_at, shards_of in cuts:
        draws = jax.random.uniform(jax.random.fold_in(jax.random.fold_in(rng, 6), axis_at), (shards_of,), jnp.float32, smallest / len(cuts), high / len(cuts))
        factor_of = factor_of * jnp.repeat(jnp.exp(draws), extent[axis_at] // shards_of).reshape((-1,) + (1,) * (len(extent) - 1 - axis_at))
    return factor_of


def centred(key, dims, deviation, limit, cuts=(), kind=jnp.bfloat16):
    level = levels(key, dims, cuts, -0.22, 0.18) if cuts else 1.0
    values = jax.random.normal(key, dims, jnp.float32) * deviation * level
    return jnp.minimum(jnp.maximum(values, -limit), limit).astype(kind)


def setup_inputs(seed: int = 0) -> dict:
    splits = jax.random.split(jax.random.key(seed), 10)
    boundary = centred(splits[0], (2, MICRO_BATCHES, REPLICA_SLOTS, SLOT_TOKENS, MODEL_WIDTH), 1.0, 6.0, ((0, 2), (3, 64)))
    seq_ids = draw_seq_ids(jax.random.fold_in(splits[9], 71), 0)
    w_qkv = centred(splits[2], (2, MODEL_WIDTH, 3 * MODEL_WIDTH), MODEL_WIDTH ** -0.5, 0.21875, ((0, 2), (1, 4)))
    w_out = centred(splits[3], (2, MODEL_WIDTH, MODEL_WIDTH), (MODEL_WIDTH // 16) ** -0.5, 0.875, ((0, 2), (1, 4)))
    w_in = centred(splits[4], (2, MODEL_WIDTH, FF), MODEL_WIDTH ** -0.5, 0.21875, ((0, 2), (1, 4)))
    w_down = centred(splits[5], (2, FF, MODEL_WIDTH), FF ** -0.5, 0.109375, ((0, 2), (1, 4)))
    gains = jnp.clip(1.0 + 0.1 * jax.random.normal(splits[6], (2, 2, MODEL_WIDTH), jnp.float32), 0.5, 1.5).astype(jnp.bfloat16)
    biases = centred(splits[7], (2, 6, MODEL_WIDTH), 0.3, 1.796875, ((0, 2), (2, 4)))
    b_in = centred(splits[8], (2, FF), 0.3, 1.796875, ((0, 2), (1, 4)))
    return {"boundary": boundary, "seq_ids": seq_ids, "w_qkv": w_qkv, "w_out": w_out, "w_in": w_in, "w_down": w_down, "gains": gains, "biases": biases, "b_in": b_in}


@jax.custom_vjp
def low(v):
    return lax.optimization_barrier(v.astype(jnp.bfloat16)).astype(jnp.float32)

@jax.custom_vjp
def low_back(v):
    return v

def low_keep(v):
    return (low(v), None)

def low_pass(kept, grad):
    return (grad,)

def back_keep(v):
    return (v, None)

def back_low(kept, grad):
    return (low(grad),)
low.defvjp(low_keep, low_pass)
low_back.defvjp(back_keep, back_low)
highest = lax.Precision.HIGHEST
epsilon = 1e-06

def matmul(left, right):
    return jnp.matmul(left, right, precision=highest)

def layer_norm(row_data, gain_row, shift_row):
    center = row_data - lax.optimization_barrier(jnp.mean(row_data, axis=-1, keepdims=True))
    spread = lax.optimization_barrier(jnp.mean(center * center, axis=-1, keepdims=True))
    return center * lax.rsqrt(spread + epsilon) * gain_row + shift_row

def encoder(layer_mats, hidden, slot_ids):
    w_qkv, w_out, w_in, w_down, gains, biases, b_in = layer_mats
    hidden_width = hidden.shape[-1]
    group_size, slot_length = (hidden.shape[0], hidden.shape[1])
    head_count = hidden_width // HD
    zero_bias = jnp.zeros((hidden_width,), hidden.dtype)
    output_projection = matmul(hidden, w_qkv) + jnp.concatenate([biases[0], zero_bias, biases[1]])
    output_projection = low(low_back(output_projection))
    split_heads = output_projection.reshape(group_size, slot_length, 3, head_count, HD)
    queries = split_heads[:, :, 0]
    keys_h = split_heads[:, :, 1]
    values_h = split_heads[:, :, 2]
    scores = jnp.einsum('gihe,gjhe->ghij', queries, keys_h, precision=highest) * HD ** (-0.5)
    scores = low_back(scores)
    visible = slot_ids[:, None, :, None] == slot_ids[:, None, None, :]
    scores = jnp.where(visible, scores, -1e+30)
    row_top = lax.optimization_barrier(jnp.max(scores, axis=-1, keepdims=True))
    raised = jnp.exp(scores - row_top)
    attn_probs = low(raised / lax.optimization_barrier(jnp.sum(raised, axis=-1, keepdims=True)))
    attended_rows = jnp.einsum('ghij,gjhe->gihe', attn_probs, values_h, precision=highest)
    attended_rows = low(low_back(attended_rows.reshape(group_size, slot_length, hidden_width)))
    attended = low_back(matmul(attended_rows, w_out) + biases[2])
    normed = low(layer_norm(hidden + attended, gains[0], biases[3]))
    inner_pre = low_back(matmul(normed, w_in) + b_in)
    activated = low(jax.nn.gelu(inner_pre, approximate=False))
    branch = low_back(matmul(activated, w_down) + biases[4])
    return layer_norm(normed + branch, gains[1], biases[5])

def network(params, hidden, slot_ids):
    first_layer = jax.tree.map(lambda array_one: array_one[0], params)
    second_layer = jax.tree.map(lambda array_one: array_one[1], params)
    middle = low(low_back(encoder(first_layer, hidden, slot_ids)))
    return encoder(second_layer, middle, slot_ids)

def reference(boundary, seq_ids, w_qkv, w_out, w_in, w_down, gains, biases, b_in):
    params = tuple((array_in.astype(jnp.float32) for array_in in (w_qkv, w_out, w_in, w_down, gains, biases, b_in)))
    hidden_width = boundary.shape[-1]
    total_slot_count = MICRO_BATCHES * REPLICA_SLOTS * N_DP
    group_size = math.gcd(total_slot_count, max(1, 4096 // SLOT))
    step_count = total_slot_count // group_size
    slot_ids = seq_ids.reshape(total_slot_count, SLOT)
    valid = (slot_ids >= 0).astype(jnp.float32)
    layer_inputs = boundary[0].astype(jnp.float32).reshape(total_slot_count, SLOT, hidden_width)
    tangent = boundary[1].astype(jnp.float32).reshape(total_slot_count, SLOT, hidden_width) * valid[:, :, None]
    layer_inputs = layer_inputs.reshape(step_count, group_size, SLOT, hidden_width)
    tangent = tangent.reshape(step_count, group_size, SLOT, hidden_width)
    slot_ids = slot_ids.reshape(step_count, group_size, SLOT)

    def accumulate(running, block_data):
        hidden, cotangent, block_ids = block_data
        layer_output, pull_back = jax.vjp(lambda pieces, row_data: network(pieces, row_data, block_ids), params, hidden)
        grad_tree, grad_rows = pull_back(cotangent)
        return (jax.tree.map(jnp.add, running, grad_tree), (layer_output, grad_rows))
    zeros_tree = jax.tree.map(jnp.zeros_like, params)
    totals, (results, grad_rows) = lax.scan(accumulate, zeros_tree, (layer_inputs, tangent, slot_ids))
    ends_out = jnp.stack([grad_rows.reshape(boundary.shape[1:]), results.reshape(boundary.shape[1:])])
    return (ends_out, totals[0], totals[1], totals[2], totals[3], totals[4], totals[5], totals[6])
```

```python
import functools

import jax
import jax.numpy as jnp
from jax import lax
from jax.experimental import pallas as pl
from jax.experimental.pallas import tpu as pltpu
from jax.sharding import Mesh, PartitionSpec as P

HD = 64
GROUP = 256
TILE = 512
CHUNK = 64
EPS = 1e-06
PEAK = 1.1e9
SWAP = [(0, 1), (1, 0)]
F32 = jnp.float32
BF16 = jnp.bfloat16
VMEM_BYTES = 48 * 1024 * 1024


def dot_nn(a, b):
    return lax.dot_general(a, b, (((1,), (0,)), ((), ())), preferred_element_type=F32)


def dot_nt(a, b):
    return lax.dot_general(a, b, (((1,), (1,)), ((), ())), preferred_element_type=F32)


def dot_tn(a, b):
    return lax.dot_general(a, b, (((0,), (0,)), ((), ())), preferred_element_type=F32)


def chunks(rows, size=CHUNK):
    return [pl.ds(start, size) for start in range(0, rows, size)]


def attend_kernel(save, h_ref, wq_ref, wk_ref, wv_ref, par_ref, idc_ref, idr_ref, *rest):
    if save:
        ctx_ref, qkv_ref, lse_ref, mask_ref = rest
    else:
        ctx_ref, mask_ref = rest
    rows = h_ref.shape[0]

    @pl.when(pl.program_id(0) == 0)
    def _():
        for r in chunks(rows):
            mask_ref[r, :] = jnp.where(idc_ref[r, :] == idr_ref[...], 0.0, -1e30)

    h = h_ref[...]
    q = (dot_nn(h, wq_ref[...]) + par_ref[2:3, :]).astype(BF16)
    k = dot_nn(h, wk_ref[...]).astype(BF16)
    v = (dot_nn(h, wv_ref[...]) + par_ref[3:4, :]).astype(BF16)
    if save:
        qkv_ref[0] = q
        qkv_ref[1] = k
        qkv_ref[2] = v
    scaled = q * jnp.asarray(HD ** (-0.5), BF16)
    values_t = v.T
    parts = []
    for n in range(GROUP // HD):
        cols = slice(n * HD, (n + 1) * HD)
        st = dot_nt(k[:, cols], scaled[:, cols]) + mask_ref[...]
        top = jnp.max(st, axis=0, keepdims=True)
        e = jnp.exp(st - top)
        total = jnp.sum(e, axis=0, keepdims=True)
        parts.append(dot_nn(values_t[cols, :], e.astype(BF16)) * (1.0 / total))
        if save:
            lse_ref[n:n + 1, :] = top + jnp.log(total)
    ctx_ref[...] = jnp.concatenate(parts, axis=0).T.astype(BF16)


def attend(h, w_qkv, par, ids, save):
    rows, width = h.shape
    steps = width // GROUP
    out_shape = [jax.ShapeDtypeStruct((rows, width), BF16)]
    out_specs = [pl.BlockSpec((rows, GROUP), lambda j: (0, j))]
    if save:
        out_shape += [
            jax.ShapeDtypeStruct((3, rows, width), BF16),
            jax.ShapeDtypeStruct((8 * steps, rows), F32),
        ]
        out_specs += [
            pl.BlockSpec((3, rows, GROUP), lambda j: (0, 0, j)),
            pl.BlockSpec((8, rows), lambda j: (j, 0)),
        ]
    return pl.pallas_call(
        functools.partial(attend_kernel, save),
        grid=(steps,),
        in_specs=[
            pl.BlockSpec((rows, width), lambda j: (0, 0)),
            pl.BlockSpec((width, GROUP), lambda j: (0, j)),
            pl.BlockSpec((width, GROUP), lambda j: (0, j + steps)),
            pl.BlockSpec((width, GROUP), lambda j: (0, j + 2 * steps)),
            pl.BlockSpec((8, GROUP), lambda j: (0, j)),
            pl.BlockSpec((rows, 1), lambda j: (0, 0)),
            pl.BlockSpec((1, rows), lambda j: (0, 0)),
        ],
        out_specs=out_specs,
        out_shape=out_shape,
        scratch_shapes=[pltpu.VMEM((rows, rows), F32)],
        compiler_params=pltpu.CompilerParams(vmem_limit_bytes=VMEM_BYTES),
        cost_estimate=pl.CostEstimate(flops=int(10 * PEAK), bytes_accessed=0, transcendentals=0),
        name="attend_save" if save else "attend",
    )(h, w_qkv, w_qkv, w_qkv, par, ids[:, None], ids[None, :])


def normalise(u):
    center = u - jnp.mean(u, axis=-1, keepdims=True)
    inv = lax.rsqrt(jnp.mean(center * center, axis=-1, keepdims=True) + EPS)
    return center * inv, inv


def feed_kernel(save, h_ref, ctx_ref, wo_ref, wi_ref, wd_ref, par_ref, bi_ref, *rest):
    if save:
        (out_ref, normed_ref, xh1_ref, inv1_ref, xh2_ref, inv2_ref, act_ref, slope_ref,
         acc_ref, inner_ref) = rest
    else:
        out_ref, normed_ref, acc_ref, inner_ref, act_ref = rest
    rows = h_ref.shape[0]
    step = pl.program_id(0)

    @pl.when(step == 0)
    def _():
        acc_ref[...] = dot_nn(ctx_ref[...], wo_ref[...])
        for r in chunks(rows):
            first = h_ref[r, :].astype(F32) + (acc_ref[r, :] + par_ref[4:5, :])
            xh, inv = normalise(first)
            normed = (xh * par_ref[0:1, :] + par_ref[5:6, :]).astype(BF16)
            normed_ref[r, :] = normed
            acc_ref[r, :] = normed.astype(F32) + par_ref[6:7, :]
            if save:
                xh1_ref[r, :] = xh
                inv1_ref[r, :] = inv

    inner_ref[...] = dot_nn(normed_ref[...], wi_ref[...])
    for r in chunks(rows):
        t = inner_ref[r, :] + bi_ref[...]
        half = 0.5 * lax.erf(t * 0.7071067811865476) + 0.5
        act_ref[r, :] = (t * half).astype(BF16)
        if save:
            bell = jnp.exp(-0.5 * (t * t)) * 0.3989422804014327
            slope_ref[r, :] = (half + t * bell).astype(BF16)
    acc_ref[...] += dot_nn(act_ref[...], wd_ref[...])

    @pl.when(step == pl.num_programs(0) - 1)
    def _():
        for r in chunks(rows):
            xh, inv = normalise(acc_ref[r, :])
            out_ref[r, :] = (xh * par_ref[1:2, :] + par_ref[7:8, :]).astype(BF16)
            if save:
                xh2_ref[r, :] = xh
                inv2_ref[r, :] = inv


def feed(h, ctx, w_out, w_in, w_down, par, b_in, save):
    rows, width = h.shape
    hidden = w_in.shape[1]
    steps = hidden // TILE
    whole = lambda j: (0, 0)
    out_shape = [
        jax.ShapeDtypeStruct((rows, width), BF16),
        jax.ShapeDtypeStruct((rows, width), BF16),
    ]
    out_specs = [pl.BlockSpec((rows, width), whole), pl.BlockSpec((rows, width), whole)]
    scratch = [pltpu.VMEM((rows, width), F32), pltpu.VMEM((rows, TILE), F32)]
    if save:
        for shape in ((rows, width), (rows, 1), (rows, width), (rows, 1)):
            out_shape.append(jax.ShapeDtypeStruct(shape, F32))
            out_specs.append(pl.BlockSpec(shape, whole))
        for _ in range(2):
            out_shape.append(jax.ShapeDtypeStruct((rows, hidden), BF16))
            out_specs.append(pl.BlockSpec((rows, TILE), lambda j: (0, j)))
    else:
        scratch.append(pltpu.VMEM((rows, TILE), BF16))
    return pl.pallas_call(
        functools.partial(feed_kernel, save),
        grid=(steps,),
        in_specs=[
            pl.BlockSpec((rows, width), whole),
            pl.BlockSpec((rows, width), whole),
            pl.BlockSpec((width, width), whole),
            pl.BlockSpec((width, TILE), lambda j: (0, j)),
            pl.BlockSpec((TILE, width), lambda j: (j, 0)),
            pl.BlockSpec((8, width), whole),
            pl.BlockSpec((1, TILE), lambda j: (0, j)),
        ],
        out_specs=out_specs,
        out_shape=out_shape,
        scratch_shapes=scratch,
        compiler_params=pltpu.CompilerParams(vmem_limit_bytes=VMEM_BYTES),
        cost_estimate=pl.CostEstimate(flops=int((15 if save else 12) * PEAK), bytes_accessed=0, transcendentals=0),
        name="feed_save" if save else "feed",
    )(h, ctx, w_out, w_in, w_down, par, b_in)


def norm_back(g, xh, inv, gain):
    weighted = g * gain
    mean = jnp.mean(weighted, axis=-1, keepdims=True)
    slope = jnp.mean(weighted * xh, axis=-1, keepdims=True)
    return (weighted - mean - xh * slope) * inv


def col_sum(rows):
    return jnp.sum(rows, axis=0, keepdims=True)


def feed_back_kernel(save, g_ref, xh2_ref, inv2_ref, xh1_ref, inv1_ref, slope_ref, wd_ref, wi_ref, wo_ref,
                     par_ref, *rest):
    if save:
        (first_ref, dctx_ref, branch_ref, inner_ref, att_ref, sums_ref, bsum_ref,
         acc_ref, dact_ref) = rest
    else:
        first_ref, dctx_ref, acc_ref, dact_ref, branch_ref, inner_ref, att_ref = rest
    rows, width = g_ref.shape
    step = pl.program_id(0)

    @pl.when(step == 0)
    def _():
        gain_sum = shift_sum = branch_sum = jnp.zeros((1, width), F32)
        for r in chunks(rows):
            g = g_ref[r, :].astype(F32)
            xh = xh2_ref[r, :]
            second = norm_back(g, xh, inv2_ref[r, :], par_ref[1:2, :])
            acc_ref[r, :] = second
            branch = second.astype(BF16)
            branch_ref[r, :] = branch
            if save:
                gain_sum += col_sum(g * xh)
                shift_sum += col_sum(g)
                branch_sum += col_sum(branch.astype(F32))
        if save:
            sums_ref[...] = jnp.zeros_like(sums_ref)
            sums_ref[1:2, :] = gain_sum
            sums_ref[7:8, :] = shift_sum
            sums_ref[6:7, :] = branch_sum

    dact_ref[...] = dot_nt(branch_ref[...], wd_ref[...])
    bin_sum = jnp.zeros((1, dact_ref.shape[1]), F32)
    for r in chunks(rows):
        inner = (dact_ref[r, :] * slope_ref[r, :].astype(F32)).astype(BF16)
        inner_ref[r, :] = inner
        if save:
            bin_sum += col_sum(inner.astype(F32))
    if save:
        bsum_ref[...] = bin_sum
    acc_ref[...] += dot_nt(inner_ref[...], wi_ref[...])

    @pl.when(step == pl.num_programs(0) - 1)
    def _():
        gain_sum = shift_sum = att_sum = jnp.zeros((1, width), F32)
        for r in chunks(rows):
            g = acc_ref[r, :]
            xh = xh1_ref[r, :]
            first = norm_back(g, xh, inv1_ref[r, :], par_ref[0:1, :])
            first_ref[r, :] = first
            att = first.astype(BF16)
            att_ref[r, :] = att
            if save:
                gain_sum += col_sum(g * xh)
                shift_sum += col_sum(g)
                att_sum += col_sum(att.astype(F32))
        if save:
            sums_ref[0:1, :] = gain_sum
            sums_ref[5:6, :] = shift_sum
            sums_ref[4:5, :] = att_sum
        dctx_ref[...] = dot_nt(att_ref[...], wo_ref[...]).astype(BF16)


def feed_back(g, kept, w_out, w_in, w_down, par, save):
    xh1, inv1, xh2, inv2, slope = kept
    rows, width = xh1.shape
    hidden = slope.shape[1]
    steps = hidden // TILE
    whole = lambda j: (0, 0)
    full = pl.BlockSpec((rows, width), whole)
    tile = pl.BlockSpec((rows, TILE), lambda j: (0, j))
    out_shape = [jax.ShapeDtypeStruct((rows, width), F32), jax.ShapeDtypeStruct((rows, width), BF16)]
    out_specs = [full, full]
    scratch = [pltpu.VMEM((rows, width), F32), pltpu.VMEM((rows, TILE), F32)]
    if save:
        out_shape += [
            jax.ShapeDtypeStruct((rows, width), BF16),
            jax.ShapeDtypeStruct((rows, hidden), BF16),
            jax.ShapeDtypeStruct((rows, width), BF16),
            jax.ShapeDtypeStruct((8, width), F32),
            jax.ShapeDtypeStruct((1, hidden), F32),
        ]
        out_specs += [
            full, tile, full,
            pl.BlockSpec((8, width), whole),
            pl.BlockSpec((1, TILE), lambda j: (0, j)),
        ]
    else:
        scratch += [pltpu.VMEM((rows, width), BF16), pltpu.VMEM((rows, TILE), BF16), pltpu.VMEM((rows, width), BF16)]
    return pl.pallas_call(
        functools.partial(feed_back_kernel, save),
        grid=(steps,),
        in_specs=[
            full, full, pl.BlockSpec((rows, 1), whole), full, pl.BlockSpec((rows, 1), whole), tile,
            pl.BlockSpec((TILE, width), lambda j: (j, 0)),
            pl.BlockSpec((width, TILE), lambda j: (0, j)),
            pl.BlockSpec((width, width), whole),
            pl.BlockSpec((8, width), whole),
        ],
        out_specs=out_specs,
        out_shape=out_shape,
        scratch_shapes=scratch,
        compiler_params=pltpu.CompilerParams(vmem_limit_bytes=VMEM_BYTES),
        cost_estimate=pl.CostEstimate(flops=int((15 if save else 12) * PEAK), bytes_accessed=0, transcendentals=0),
        name="feed_back_save" if save else "feed_back",
    )(g, xh2, inv2, xh1, inv1, slope, w_down, w_in, w_out, par)


def attend_back_kernel(save, qkv_ref, dctx_ref, lse_ref, idc_ref, idr_ref, wq_ref, wk_ref, wv_ref, first_ref, after_ref, *rest):
    if save:
        dh_ref, dqkv_ref, sums_ref, mask_ref, acc_ref = rest
    else:
        dh_ref, mask_ref, acc_ref = rest
    rows = first_ref.shape[0]
    step = pl.program_id(0)

    @pl.when(step == 0)
    def _():
        for r in chunks(rows):
            mask_ref[r, :] = jnp.where(idc_ref[r, :] == idr_ref[...], 0.0, -1e30)
        acc_ref[...] = first_ref[...]

    scale = HD ** (-0.5)
    q = qkv_ref[0] * jnp.asarray(scale, BF16)
    k = qkv_ref[1]
    v = qkv_ref[2]
    dctx = dctx_ref[...]
    keys_t = k.T
    dq_t = []
    dk = []
    dv = []
    for n in range(GROUP // HD):
        cols = slice(n * HD, (n + 1) * HD)
        lse = lse_ref[n:n + 1, :]
        st = dot_nt(k[:, cols], q[:, cols]) + mask_ref[...]
        pt = jnp.exp(st - lse)
        dpt = dot_nt(v[:, cols], dctx[:, cols])
        row = jnp.sum(pt * dpt, axis=0, keepdims=True)
        dst = (pt * (dpt - row)).astype(BF16)
        dv.append(dot_nn(pt.astype(BF16), dctx[:, cols]))
        dk.append(dot_nn(dst, q[:, cols]))
        dq_t.append(dot_nn(keys_t[cols, :], dst))
    dq = (jnp.concatenate(dq_t, axis=0).T * scale).astype(BF16)
    dk = jnp.concatenate(dk, axis=1).astype(BF16)
    dv = jnp.concatenate(dv, axis=1).astype(BF16)
    if save:
        for n, part in enumerate((dq, dk, dv)):
            offset = n * first_ref.shape[1] + step * GROUP
            dqkv_ref[:, pl.ds(pl.multiple_of(offset, GROUP), GROUP)] = part
        sums_ref[...] = jnp.zeros_like(sums_ref)
        sums_ref[2:3, :] = col_sum(dq.astype(F32))
        sums_ref[3:4, :] = col_sum(dv.astype(F32))
    acc_ref[...] += dot_nt(dq, wq_ref[...]) + dot_nt(dk, wk_ref[...]) + dot_nt(dv, wv_ref[...])

    @pl.when(step == pl.num_programs(0) - 1)
    def _():
        dh_ref[...] = acc_ref[...].astype(BF16)


def attend_back(qkv, dctx, lse, ids, w_qkv, first, after, save):
    rows, width = first.shape
    steps = width // GROUP
    whole = lambda j: (0, 0)
    full = pl.BlockSpec((rows, width), whole)
    out_shape = [jax.ShapeDtypeStruct((rows, width), BF16)]
    out_specs = [full]
    if save:
        out_shape += [jax.ShapeDtypeStruct((rows, 3 * width), BF16), jax.ShapeDtypeStruct((8, width), F32)]
        out_specs += [
            pl.BlockSpec((rows, 3 * width), whole),
            pl.BlockSpec((8, GROUP), lambda j: (0, j)),
        ]
    return pl.pallas_call(
        functools.partial(attend_back_kernel, save),
        grid=(steps,),
        in_specs=[
            pl.BlockSpec((3, rows, GROUP), lambda j: (0, 0, j)),
            pl.BlockSpec((rows, GROUP), lambda j: (0, j)),
            pl.BlockSpec((8, rows), lambda j: (j, 0)),
            pl.BlockSpec((rows, 1), whole),
            pl.BlockSpec((1, rows), whole),
            pl.BlockSpec((width, GROUP), lambda j: (0, j)),
            pl.BlockSpec((width, GROUP), lambda j: (0, j + steps)),
            pl.BlockSpec((width, GROUP), lambda j: (0, j + 2 * steps)),
            full,
            pl.BlockSpec(memory_space=pl.ANY),
        ],
        out_specs=out_specs,
        out_shape=out_shape,
        scratch_shapes=[pltpu.VMEM((rows, rows), F32), pltpu.VMEM((rows, width), F32)],
        compiler_params=pltpu.CompilerParams(vmem_limit_bytes=VMEM_BYTES),
        cost_estimate=pl.CostEstimate(flops=int(14 * PEAK), bytes_accessed=0, transcendentals=0),
        name="attend_back_save" if save else "attend_back",
    )(qkv, dctx, lse, ids[:, None], ids[None, :], w_qkv, w_qkv, w_qkv, first, after)


def turned(block, axis, by):
    count = lax.axis_size(axis)
    return lax.ppermute(block, axis, [(i, (i + by) % count) for i in range(count)])


def around(block, axis):
    return [block] + [turned(block, axis, d) for d in range(1, lax.axis_size(axis))]


def place_kernel(plan, at_ref, *refs):
    *sources, out_ref, sems = refs
    copies = []
    for n, (ref, (pick, where)) in enumerate(zip(sources, plan)):
        copies.append(pltpu.make_async_copy(pick(ref), where(out_ref, at_ref), sems.at[n]))
    for copy in copies:
        copy.start()
    for copy in copies:
        copy.wait()


def place(at, pieces, shape, name):
    nbytes = 4 * sum(p[0].size for p in pieces)
    anywhere = pl.BlockSpec(memory_space=pl.ANY)
    return pl.pallas_call(
        functools.partial(place_kernel, [p[1:] for p in pieces]),
        in_specs=[pl.BlockSpec(memory_space=pltpu.SMEM)] + [anywhere] * len(pieces),
        out_specs=pl.BlockSpec(memory_space=pltpu.VMEM),
        out_shape=jax.ShapeDtypeStruct(shape, BF16),
        scratch_shapes=[pltpu.SemaphoreType.DMA((len(pieces),))],
        compiler_params=pltpu.CompilerParams(vmem_limit_bytes=VMEM_BYTES),
        cost_estimate=pl.CostEstimate(flops=0, bytes_accessed=nbytes, transcendentals=0),
        name=name,
    )(at, *[p[0] for p in pieces])


X, Y, Z, C = range(4)


def gather_x(at, shard, name):
    rows, cols = shard.shape
    half = rows // 2
    own = lax.dynamic_slice_in_dim(shard, at[C] * half, half, 0)
    pieces = []
    for d, block in enumerate(around(own, "fsdp")):
        for e, part in enumerate(around(block, "core")):
            pieces.append((
                part,
                lambda ref: ref,
                lambda out, at, d=d, e=e: out.at[(at[X] + 4 - d) % 4, (at[C] + e) % 2],
            ))
    return place(at, pieces, (4, 2, half, cols), name).reshape(4 * rows, cols)


def gather_xy(at, shard, name):
    rows, cols = shard.shape
    half, part = rows // 2, cols // 4
    own = lax.dynamic_slice(shard, (at[C] * half, at[Y] * part), (half, part))
    block = jnp.stack(around(own, "fsdp"))
    pieces = []
    for g, moved in enumerate(around(block, "y")):
        for e, swapped in enumerate(around(moved, "core")):
            for d in range(4):
                pieces.append((
                    swapped,
                    lambda ref, d=d: ref.at[d],
                    lambda out, at, d=d, e=e, g=g: out.at[
                        (at[X] + 4 - d) % 4, (at[C] + e) % 2, :,
                        pl.ds(pl.multiple_of((at[Y] + 4 - g) % 4 * part, 128), part),
                    ],
                ))
    return place(at, pieces, (4, 2, half, cols), name).reshape(4 * rows, cols)


def gather_xz(at, shard, name):
    rows, cols = shard.shape
    part = rows // 4
    own = lax.dynamic_slice_in_dim(shard, (at[C] * 2 + at[Z]) * part, part, 0)
    block = jnp.stack(around(own, "fsdp"))
    pieces = []
    for g, moved in enumerate(around(block, "zl")):
        for e, swapped in enumerate(around(moved, "core")):
            for d in range(4):
                pieces.append((
                    swapped,
                    lambda ref, d=d: ref.at[d],
                    lambda out, at, d=d, e=e, g=g: out.at[
                        (at[X] + 4 - d) % 4, (at[C] + e) % 2, (at[Z] + g) % 2
                    ],
                ))
    return place(at, pieces, (4, 2, 2, part, cols), name).reshape(4 * rows, cols)


def core_sum(left, right):
    core = lax.axis_index("core")
    size = right.shape[1] // 2
    send = dot_tn(left, lax.dynamic_slice_in_dim(right, (1 - core) * size, size, 1)).astype(BF16)
    got = lax.ppermute(send, "core", SWAP)
    keep = dot_tn(left, lax.dynamic_slice_in_dim(right, core * size, size, 1))
    return (keep + got.astype(F32)).astype(BF16)


def scatter_sum(block, axis, dim):
    count = lax.axis_size(axis)
    at = lax.axis_index(axis)
    total = lax.dynamic_index_in_dim(block, at, dim, keepdims=False).astype(F32)
    for d in range(1, count):
        send = lax.dynamic_index_in_dim(block, (at + d) % count, dim, keepdims=False)
        total += turned(send, axis, d).astype(F32)
    return total.astype(BF16)


def exchange_sum(block, axis):
    moved = lax.all_to_all(block, axis, 0, 0, tiled=True)
    return jnp.sum(moved.astype(F32), axis=0).astype(BF16)


def finish(part):
    part = (part.astype(F32) + lax.ppermute(part, "zl", SWAP).astype(F32)).astype(BF16)
    mine = lax.all_to_all(jnp.broadcast_to(part[None], (4,) + part.shape), "y", 0, 0, tiled=True)
    other = lax.ppermute(mine, "core", SWAP)
    first = lax.axis_index("core") == 0
    return jnp.where(first, mine, other), jnp.where(first, other, mine)


def joined(halves):
    return jnp.concatenate(halves, axis=-1).astype(F32)


def body(boundary, seq_ids, w_qkv, w_out, w_in, w_down, gains, biases, b_in):
    section = lax.axis_index("section")
    shard = lax.axis_index("fsdp")
    own = boundary[0, :, 0]
    micro, own_rows, width = own.shape
    shards = lax.axis_size("fsdp")
    rows = own_rows * shards
    hidden = b_in.shape[1] * shards
    piece = width // shards
    at = jnp.stack([lax.axis_index(name) for name in ("fsdp", "y", "zl", "core")]).astype(jnp.int32)

    full_qkv = gather_x(at, w_qkv[0], "place_qkv")

    small = jnp.concatenate([gains[0], biases[0], b_in[0].reshape(-1, piece)])
    small = jnp.pad(small.reshape(-1, width), ((0, 13), (0, 0)))
    padded = jnp.concatenate([own, jnp.zeros((shards - micro,) + own.shape[1:], BF16)])
    padded = jnp.concatenate([padded, jnp.broadcast_to(small[None], (shards,) + small.shape)], axis=1)
    padded = lax.all_to_all(padded, "fsdp", 0, 0, tiled=True)
    slot = padded[:, :own_rows].reshape(rows, width)
    small = padded[:, own_rows:own_rows + 3].reshape(shards, 12, piece)
    par = jnp.swapaxes(small[:, :8], 0, 1).reshape(8, width).astype(F32)
    bias_in = small[:, 8:].reshape(1, hidden).astype(F32)
    ids = lax.dynamic_index_in_dim(seq_ids[:, 0], jnp.minimum(shard, micro - 1), 0, keepdims=False)

    full_in = gather_xy(at, w_in[0], "place_in")
    full_down = gather_xz(at, w_down[0], "place_down")
    full_out = gather_x(at, w_out[0], "place_out")

    (ctx,) = attend(slot, full_qkv, par, ids, False)
    middle = feed(slot, ctx, full_out, full_in, full_down, par, bias_in, False)[0]
    arrived = lax.ppermute(middle, "section", [(0, 1)])

    h = jnp.where(section == 0, slot, arrived)
    ctx, qkv, lse = attend(h, full_qkv, par, ids, True)
    out, normed, xh1, inv1, xh2, inv2, act, slope = feed(
        h, ctx, full_out, full_in, full_down, par, bias_in, True
    )
    kept = (xh1, inv1, xh2, inv2, slope)

    cot = jnp.where(ids[:, None] >= 0, slot, jnp.zeros_like(slot))
    first, dctx = feed_back(cot, kept, full_out, full_in, full_down, par, False)
    (d_middle,) = attend_back(qkv, dctx, lse, ids, full_qkv, first, dctx, False)
    returned = lax.ppermute(d_middle, "section", [(1, 0)])

    g = jnp.where(section == 0, returned, cot)
    first, dctx, branch, inner, att, sums, bin_sums = feed_back(
        g, kept, full_out, full_in, full_down, par, True
    )
    g_down = core_sum(act, branch).reshape(4, 4, 192, 384)
    g_in = core_sum(normed, inner).reshape(4, 192, 1536)
    g_out = core_sum(ctx, att).reshape(4, 192, 384)
    p_down = scatter_sum(g_down, "y", 1)
    p_in = exchange_sum(g_in, "fsdp")
    p_out = exchange_sum(g_out, "fsdp")
    after = jnp.stack([g_down[0, 0, :8, :128], g_in[0, :8, :128]])
    d_h, dqkv, more = attend_back(qkv, dctx, lse, ids, full_qkv, first, after, True)

    p_down = exchange_sum(p_down, "fsdp")
    p_in = exchange_sum(jnp.concatenate([p_in, p_out], axis=1).reshape(4, 48, 1920), "y")

    vec = (sums + more).reshape(8, shards, piece)
    vec = jnp.concatenate([jnp.swapaxes(vec, 0, 1), bin_sums.reshape(shards, -1, piece)], axis=1)
    vec = vec.reshape(shards, 2, -1).astype(BF16)
    core = lax.axis_index("core")
    vec_keep = lax.dynamic_index_in_dim(vec, core, 1, keepdims=False)
    vec_send = lax.dynamic_index_in_dim(vec, 1 - core, 1, keepdims=False)
    vec = (vec_keep.astype(F32) + lax.ppermute(vec_send, "core", SWAP).astype(F32)).astype(BF16)
    vec = jnp.pad(vec.reshape(4, 4, 1, 288), ((0, 0), (0, 0), (0, 7), (0, 864)))

    g_qkv = core_sum(h, dqkv).reshape(4, 4, 48, 1152)
    g_qkv = jnp.concatenate([g_qkv, vec], axis=2).reshape(4, 224, 1152)
    p_qkv = exchange_sum(g_qkv, "fsdp")
    p_qkv = exchange_sum(p_qkv.reshape(4, 56, 1152), "y")

    f_down = finish(p_down)
    f_in = finish(p_in)
    f_qkv = finish(p_qkv)
    g_out = joined([half[:, :, 1536:] for half in f_in])
    g_in = joined([half[:, :, :1536] for half in f_in])
    g_qkv = joined([half[:, :48] for half in f_qkv])
    vec = jnp.stack([half[:, 48, :288] for half in f_qkv]).reshape(12, piece).astype(F32)

    ends = jnp.where(section == 0, d_h, out).reshape(shards, own_rows, width)
    ends = lax.all_to_all(ends, "fsdp", 0, 0, tiled=True)[:micro].astype(F32)
    return (
        ends[None, :, None],
        g_qkv.reshape(1, 192, -1),
        g_out.reshape(1, 192, -1),
        g_in.reshape(1, 192, -1),
        joined(f_down).reshape(1, 768, -1),
        vec[None, :2],
        vec[None, 2:8],
        vec[None, 8:].reshape(1, -1),
    )


def solution(mesh):
    fine = Mesh(mesh.devices.reshape(2, 4, 2, 4, 2), ("section", "fsdp", "zl", "y", "core"))
    dp = ("zl", "y", "core")
    in_specs = (
        P("section", None, None, dp + ("fsdp",), None),
        P(None, None, dp),
        P("section", "fsdp", None),
        P("section", "fsdp", None),
        P("section", "fsdp", None),
        P("section", "fsdp", None),
        P("section", None, "fsdp"),
        P("section", None, "fsdp"),
        P("section", "fsdp"),
    )
    out_specs = (
        P("section", None, None, dp + ("fsdp",), None),
        P("section", "fsdp", None),
        P("section", "fsdp", None),
        P("section", "fsdp", None),
        P("section", "fsdp", None),
        P("section", None, "fsdp"),
        P("section", None, "fsdp"),
        P("section", "fsdp"),
    )
    return jax.shard_map(body, mesh=fine, in_specs=in_specs, out_specs=out_specs, check_vma=False)
```

```python
import functools

import jax
import jax.numpy as jnp
from jax import lax
from jax.experimental import pallas as pl
from jax.experimental.pallas import tpu as pltpu
from jax.sharding import Mesh, PartitionSpec as P

HD = 64
GROUP = 256
TILE = 768
CHUNK = 64
EPS = 1e-06
PEAK = 1.1e9
SWAP = [(0, 1), (1, 0)]
F32 = jnp.float32
BF16 = jnp.bfloat16
VMEM_BYTES = 48 * 1024 * 1024


def dot_nn(a, b):
    return lax.dot_general(a, b, (((1,), (0,)), ((), ())), preferred_element_type=F32)


def dot_nt(a, b):
    return lax.dot_general(a, b, (((1,), (1,)), ((), ())), preferred_element_type=F32)


def dot_tn(a, b):
    return lax.dot_general(a, b, (((0,), (0,)), ((), ())), preferred_element_type=F32)


def chunks(rows, size=CHUNK):
    return [pl.ds(start, size) for start in range(0, rows, size)]


def attend_kernel(save, h_ref, wq_ref, wk_ref, wv_ref, par_ref, idc_ref, idr_ref, *rest):
    if save:
        ctx_ref, qkv_ref, lse_ref, mask_ref = rest
    else:
        ctx_ref, mask_ref = rest
    rows = h_ref.shape[0]

    @pl.when(pl.program_id(0) == 0)
    def _():
        for r in chunks(rows):
            mask_ref[r, :] = jnp.where(idc_ref[r, :] == idr_ref[...], 0.0, -1e30)

    h = h_ref[...]
    q = (dot_nn(h, wq_ref[...]) + par_ref[2:3, :]).astype(BF16)
    k = dot_nn(h, wk_ref[...]).astype(BF16)
    v = (dot_nn(h, wv_ref[...]) + par_ref[3:4, :]).astype(BF16)
    if save:
        qkv_ref[0] = q
        qkv_ref[1] = k
        qkv_ref[2] = v
    scaled = q * jnp.asarray(HD ** (-0.5), BF16)
    values_t = v.T
    parts = []
    for n in range(GROUP // HD):
        cols = slice(n * HD, (n + 1) * HD)
        st = dot_nt(k[:, cols], scaled[:, cols]) + mask_ref[...]
        top = jnp.max(st, axis=0, keepdims=True)
        e = jnp.exp(st - top)
        total = jnp.sum(e, axis=0, keepdims=True)
        parts.append(dot_nn(values_t[cols, :], e.astype(BF16)) * (1.0 / total))
        if save:
            lse_ref[n:n + 1, :] = top + jnp.log(total)
    ctx_ref[...] = jnp.concatenate(parts, axis=0).T.astype(BF16)


def attend(h, w_qkv, par, ids, save):
    rows, width = h.shape
    steps = width // GROUP
    out_shape = [jax.ShapeDtypeStruct((rows, width), BF16)]
    out_specs = [pl.BlockSpec((rows, GROUP), lambda j: (0, j))]
    if save:
        out_shape += [
            jax.ShapeDtypeStruct((3, rows, width), BF16),
            jax.ShapeDtypeStruct((8 * steps, rows), F32),
        ]
        out_specs += [
            pl.BlockSpec((3, rows, GROUP), lambda j: (0, 0, j)),
            pl.BlockSpec((8, rows), lambda j: (j, 0)),
        ]
    return pl.pallas_call(
        functools.partial(attend_kernel, save),
        grid=(steps,),
        in_specs=[
            pl.BlockSpec((rows, width), lambda j: (0, 0)),
            pl.BlockSpec((width, GROUP), lambda j: (0, j)),
            pl.BlockSpec((width, GROUP), lambda j: (0, j + steps)),
            pl.BlockSpec((width, GROUP), lambda j: (0, j + 2 * steps)),
            pl.BlockSpec((8, GROUP), lambda j: (0, j)),
            pl.BlockSpec((rows, 1), lambda j: (0, 0)),
            pl.BlockSpec((1, rows), lambda j: (0, 0)),
        ],
        out_specs=out_specs,
        out_shape=out_shape,
        scratch_shapes=[pltpu.VMEM((rows, rows), F32)],
        compiler_params=pltpu.CompilerParams(vmem_limit_bytes=VMEM_BYTES),
        cost_estimate=pl.CostEstimate(flops=int(10 * PEAK), bytes_accessed=0, transcendentals=0),
        name="attend_save" if save else "attend",
    )(h, w_qkv, w_qkv, w_qkv, par, ids[:, None], ids[None, :])


def normalise(u):
    center = u - jnp.mean(u, axis=-1, keepdims=True)
    inv = lax.rsqrt(jnp.mean(center * center, axis=-1, keepdims=True) + EPS)
    return center * inv, inv


def feed_kernel(save, h_ref, ctx_ref, wo_ref, wi_ref, wd_ref, par_ref, bi_ref, *rest):
    if save:
        (out_ref, normed_ref, xh1_ref, inv1_ref, xh2_ref, inv2_ref, slope_ref, kept_ref,
         acc_ref, inner_ref, act_ref) = rest
    else:
        out_ref, normed_ref, acc_ref, inner_ref, act_ref = rest
    rows = h_ref.shape[0]
    step = pl.program_id(0)

    @pl.when(step == 0)
    def _():
        acc_ref[...] = dot_nn(ctx_ref[...], wo_ref[...])
        for r in chunks(rows):
            first = h_ref[r, :].astype(F32) + (acc_ref[r, :] + par_ref[4:5, :])
            xh, inv = normalise(first)
            normed = (xh * par_ref[0:1, :] + par_ref[5:6, :]).astype(BF16)
            normed_ref[r, :] = normed
            acc_ref[r, :] = normed.astype(F32) + par_ref[6:7, :]
            if save:
                xh1_ref[r, :] = xh
                inv1_ref[r, :] = inv

    inner_ref[...] = dot_nn(normed_ref[...], wi_ref[...])
    for r in chunks(rows):
        t = inner_ref[r, :] + bi_ref[...]
        half = 0.5 * lax.erf(t * 0.7071067811865476) + 0.5
        act = (t * half).astype(BF16)
        act_ref[r, :] = act
        if save:
            kept_ref[0, r, :] = act[:, :TILE // 2]
            kept_ref[1, r, :] = act[:, TILE // 2:]
            bell = jnp.exp(-0.5 * (t * t)) * 0.3989422804014327
            slope_ref[r, :] = (half + t * bell).astype(BF16)
    acc_ref[...] += dot_nn(act_ref[...], wd_ref[...])

    @pl.when(step == pl.num_programs(0) - 1)
    def _():
        for r in chunks(rows):
            xh, inv = normalise(acc_ref[r, :])
            out_ref[r, :] = (xh * par_ref[1:2, :] + par_ref[7:8, :]).astype(BF16)
            if save:
                xh2_ref[r, :] = xh
                inv2_ref[r, :] = inv


def feed(h, ctx, w_out, w_in, w_down, par, b_in, save):
    rows, width = h.shape
    hidden = w_in.shape[1]
    steps = hidden // TILE
    whole = lambda j: (0, 0)
    out_shape = [
        jax.ShapeDtypeStruct((rows, width), BF16),
        jax.ShapeDtypeStruct((rows, width), BF16),
    ]
    out_specs = [pl.BlockSpec((rows, width), whole), pl.BlockSpec((rows, width), whole)]
    scratch = [pltpu.VMEM((rows, width), F32), pltpu.VMEM((rows, TILE), F32)]
    if save:
        for shape in ((rows, width), (rows, 1), (rows, width), (rows, 1)):
            out_shape.append(jax.ShapeDtypeStruct(shape, F32))
            out_specs.append(pl.BlockSpec(shape, whole))
        out_shape.append(jax.ShapeDtypeStruct((rows, hidden), BF16))
        out_specs.append(pl.BlockSpec((rows, TILE), lambda j: (0, j)))
        out_shape.append(jax.ShapeDtypeStruct((2, rows, hidden // 2), BF16))
        out_specs.append(pl.BlockSpec((2, rows, TILE // 2), lambda j: (0, 0, j)))
    scratch.append(pltpu.VMEM((rows, TILE), BF16))
    return pl.pallas_call(
        functools.partial(feed_kernel, save),
        grid=(steps,),
        in_specs=[
            pl.BlockSpec((rows, width), whole),
            pl.BlockSpec((rows, width), whole),
            pl.BlockSpec((width, width), whole),
            pl.BlockSpec((width, TILE), lambda j: (0, j)),
            pl.BlockSpec((TILE, width), lambda j: (j, 0)),
            pl.BlockSpec((8, width), whole),
            pl.BlockSpec((1, TILE), lambda j: (0, j)),
        ],
        out_specs=out_specs,
        out_shape=out_shape,
        scratch_shapes=scratch,
        compiler_params=pltpu.CompilerParams(vmem_limit_bytes=VMEM_BYTES),
        cost_estimate=pl.CostEstimate(flops=int((15 if save else 12) * PEAK), bytes_accessed=0, transcendentals=0),
        name="feed_save" if save else "feed",
    )(h, ctx, w_out, w_in, w_down, par, b_in)


def norm_back(g, xh, inv, gain):
    weighted = g * gain
    mean = jnp.mean(weighted, axis=-1, keepdims=True)
    slope = jnp.mean(weighted * xh, axis=-1, keepdims=True)
    return (weighted - mean - xh * slope) * inv


def col_sum(rows):
    return jnp.sum(rows, axis=0, keepdims=True)


def norm_back_kernel(g_ref, xh_ref, inv_ref, par_ref, *rest):
    second_ref, branch_ref, sums_ref = rest[-3:]
    rows, width = g_ref.shape
    gain_sum = shift_sum = branch_sum = jnp.zeros((1, width), F32)
    for r in chunks(rows):
        g = g_ref[r, :].astype(F32)
        xh = xh_ref[r, :]
        second = norm_back(g, xh, inv_ref[r, :], par_ref[1:2, :])
        second_ref[r, :] = second
        branch = second.astype(BF16)
        branch_ref[r, :] = branch
        gain_sum += col_sum(g * xh)
        shift_sum += col_sum(g)
        branch_sum += col_sum(branch.astype(F32))
    sums_ref[...] = jnp.zeros_like(sums_ref)
    sums_ref[1:2, :] = gain_sum
    sums_ref[7:8, :] = shift_sum
    sums_ref[6:7, :] = branch_sum


def second_back(g, xh, inv, par, behind):
    rows, width = xh.shape
    vmem = pl.BlockSpec(memory_space=pltpu.VMEM)
    return pl.pallas_call(
        norm_back_kernel,
        in_specs=[vmem] * 4 + [pl.BlockSpec(memory_space=pl.ANY)] * len(behind),
        out_specs=[vmem] * 3,
        out_shape=[
            jax.ShapeDtypeStruct((rows, width), F32),
            jax.ShapeDtypeStruct((rows, width), BF16),
            jax.ShapeDtypeStruct((8, width), F32),
        ],
        compiler_params=pltpu.CompilerParams(vmem_limit_bytes=VMEM_BYTES),
        cost_estimate=pl.CostEstimate(flops=int(3 * PEAK), bytes_accessed=0, transcendentals=0),
        name="second_back",
    )(g, xh, inv, par, *behind)


def feed_back_kernel(save, g_ref, xh2_ref, inv2_ref, xh1_ref, inv1_ref, slope_ref, wd_ref, wi_ref, wo_ref,
                     par_ref, *rest):
    if save:
        first_ref, dctx_ref, inner_ref, att_ref, sums_ref, bsum_ref, acc_ref, dact_ref = rest[1:]
        branch_ref = xh2_ref
    else:
        first_ref, dctx_ref, acc_ref, dact_ref, branch_ref, inner_ref, att_ref = rest
    rows, width = g_ref.shape
    step = pl.program_id(0)

    @pl.when(step == 0)
    def _():
        if save:
            acc_ref[...] = g_ref[...]
            sums_ref[...] = jnp.zeros_like(sums_ref)
        else:
            for r in chunks(rows):
                g = g_ref[r, :].astype(F32)
                second = norm_back(g, xh2_ref[r, :], inv2_ref[r, :], par_ref[1:2, :])
                acc_ref[r, :] = second
                branch_ref[r, :] = second.astype(BF16)

    dact_ref[...] = dot_nt(branch_ref[...], wd_ref[...])
    bin_sum = jnp.zeros((1, dact_ref.shape[1]), F32)
    for r in chunks(rows):
        inner = (dact_ref[r, :] * slope_ref[r, :].astype(F32)).astype(BF16)
        if save:
            inner_ref[0, r, :] = inner
        else:
            inner_ref[r, :] = inner
        if save:
            bin_sum += col_sum(inner.astype(F32))
    if save:
        bsum_ref[...] = bin_sum
    acc_ref[...] += dot_nt(inner_ref[0] if save else inner_ref[...], wi_ref[...])

    @pl.when(step == pl.num_programs(0) - 1)
    def _():
        gain_sum = shift_sum = att_sum = jnp.zeros((1, width), F32)
        for r in chunks(rows):
            g = acc_ref[r, :]
            xh = xh1_ref[r, :]
            first = norm_back(g, xh, inv1_ref[r, :], par_ref[0:1, :])
            first_ref[r, :] = first
            att = first.astype(BF16)
            att_ref[r, :] = att
            if save:
                gain_sum += col_sum(g * xh)
                shift_sum += col_sum(g)
                att_sum += col_sum(att.astype(F32))
        if save:
            sums_ref[0:1, :] = gain_sum
            sums_ref[5:6, :] = shift_sum
            sums_ref[4:5, :] = att_sum
        dctx_ref[...] = dot_nt(att_ref[...], wo_ref[...]).astype(BF16)


def feed_back(g, kept, w_out, w_in, w_down, par, save, behind=()):
    xh1, inv1, xh2, inv2, slope = kept
    rows, width = xh1.shape
    hidden = slope.shape[1]
    steps = hidden // TILE
    whole = lambda j: (0, 0)
    full = pl.BlockSpec((rows, width), whole)
    tile = pl.BlockSpec((rows, TILE), lambda j: (0, j))
    out_shape = [jax.ShapeDtypeStruct((rows, width), F32), jax.ShapeDtypeStruct((rows, width), BF16)]
    out_specs = [full, full]
    scratch = [pltpu.VMEM((rows, width), F32), pltpu.VMEM((rows, TILE), F32)]
    if save:
        out_shape += [
            jax.ShapeDtypeStruct((2, rows, hidden // 2), BF16),
            jax.ShapeDtypeStruct((rows, width), BF16),
            jax.ShapeDtypeStruct((8, width), F32),
            jax.ShapeDtypeStruct((1, hidden), F32),
        ]
        out_specs += [
            pl.BlockSpec((1, rows, TILE), lambda j: (j // (steps // 2), 0, j % (steps // 2))), full,
            pl.BlockSpec((8, width), whole),
            pl.BlockSpec((1, TILE), lambda j: (0, j)),
        ]
    else:
        scratch += [pltpu.VMEM((rows, width), BF16), pltpu.VMEM((rows, TILE), BF16), pltpu.VMEM((rows, width), BF16)]
    return pl.pallas_call(
        functools.partial(feed_back_kernel, save),
        grid=(steps,),
        in_specs=[
            full, full, pl.BlockSpec((rows, 1), whole), full, pl.BlockSpec((rows, 1), whole), tile,
            pl.BlockSpec((TILE, width), lambda j: (j, 0)),
            pl.BlockSpec((width, TILE), lambda j: (0, j)),
            pl.BlockSpec((width, width), whole),
            pl.BlockSpec((8, width), whole),
        ] + [pl.BlockSpec(memory_space=pl.ANY)] * len(behind),
        out_specs=out_specs,
        out_shape=out_shape,
        scratch_shapes=scratch,
        compiler_params=pltpu.CompilerParams(vmem_limit_bytes=VMEM_BYTES),
        cost_estimate=pl.CostEstimate(flops=int((15 if save else 12) * PEAK), bytes_accessed=0, transcendentals=0),
        name="feed_back_save" if save else "feed_back",
    )(g, xh2, inv2, xh1, inv1, slope, w_down, w_in, w_out, par, *behind)


def attend_back_kernel(save, qkv_ref, dctx_ref, lse_ref, idc_ref, idr_ref, wq_ref, wk_ref, wv_ref, first_ref, *rest):
    if save:
        dh_ref, dqkv_ref, sums_ref, mask_ref, acc_ref = rest[-5:]
    else:
        dh_ref, mask_ref, acc_ref = rest
    rows = first_ref.shape[0]
    step = pl.program_id(0)

    @pl.when(step == 0)
    def _():
        for r in chunks(rows):
            mask_ref[r, :] = jnp.where(idc_ref[r, :] == idr_ref[...], 0.0, -1e30)
        acc_ref[...] = first_ref[...]

    scale = HD ** (-0.5)
    q = qkv_ref[0] * jnp.asarray(scale, BF16)
    k = qkv_ref[1]
    v = qkv_ref[2]
    dctx = dctx_ref[...]
    keys_t = k.T
    dq_t = []
    dk = []
    dv = []
    for n in range(GROUP // HD):
        cols = slice(n * HD, (n + 1) * HD)
        lse = lse_ref[n:n + 1, :]
        st = dot_nt(k[:, cols], q[:, cols]) + mask_ref[...]
        pt = jnp.exp(st - lse)
        dpt = dot_nt(v[:, cols], dctx[:, cols])
        row = jnp.sum(pt * dpt, axis=0, keepdims=True)
        dst = (pt * (dpt - row)).astype(BF16)
        dv.append(dot_nn(pt.astype(BF16), dctx[:, cols]))
        dk.append(dot_nn(dst, q[:, cols]))
        dq_t.append(dot_nn(keys_t[cols, :], dst))
    dq = (jnp.concatenate(dq_t, axis=0).T * scale).astype(BF16)
    dk = jnp.concatenate(dk, axis=1).astype(BF16)
    dv = jnp.concatenate(dv, axis=1).astype(BF16)
    if save:
        for n, part in enumerate((dq, dk, dv)):
            offset = n * first_ref.shape[1] + step * GROUP
            dqkv_ref[:, pl.ds(pl.multiple_of(offset, GROUP), GROUP)] = part
        sums_ref[...] = jnp.zeros_like(sums_ref)
        sums_ref[2:3, :] = col_sum(dq.astype(F32))
        sums_ref[3:4, :] = col_sum(dv.astype(F32))
    acc_ref[...] += dot_nt(dq, wq_ref[...]) + dot_nt(dk, wk_ref[...]) + dot_nt(dv, wv_ref[...])

    @pl.when(step == pl.num_programs(0) - 1)
    def _():
        dh_ref[...] = acc_ref[...].astype(BF16)


def attend_back(qkv, dctx, lse, ids, w_qkv, first, save, behind=()):
    rows, width = first.shape
    steps = width // GROUP
    whole = lambda j: (0, 0)
    full = pl.BlockSpec((rows, width), whole)
    out_shape = [jax.ShapeDtypeStruct((rows, width), BF16)]
    out_specs = [full]
    if save:
        out_shape += [jax.ShapeDtypeStruct((rows, 3 * width), BF16), jax.ShapeDtypeStruct((8, width), F32)]
        out_specs += [
            pl.BlockSpec((rows, 3 * width), whole),
            pl.BlockSpec((8, GROUP), lambda j: (0, j)),
        ]
    return pl.pallas_call(
        functools.partial(attend_back_kernel, save),
        grid=(steps,),
        in_specs=[
            pl.BlockSpec((3, rows, GROUP), lambda j: (0, 0, j)),
            pl.BlockSpec((rows, GROUP), lambda j: (0, j)),
            pl.BlockSpec((8, rows), lambda j: (j, 0)),
            pl.BlockSpec((rows, 1), whole),
            pl.BlockSpec((1, rows), whole),
            pl.BlockSpec((width, GROUP), lambda j: (0, j)),
            pl.BlockSpec((width, GROUP), lambda j: (0, j + steps)),
            pl.BlockSpec((width, GROUP), lambda j: (0, j + 2 * steps)),
            full,
        ] + [pl.BlockSpec(memory_space=pl.ANY)] * len(behind),
        out_specs=out_specs,
        out_shape=out_shape,
        scratch_shapes=[pltpu.VMEM((rows, rows), F32), pltpu.VMEM((rows, width), F32)],
        compiler_params=pltpu.CompilerParams(vmem_limit_bytes=VMEM_BYTES),
        cost_estimate=pl.CostEstimate(flops=int(14 * PEAK), bytes_accessed=0, transcendentals=0),
        name="attend_back_save" if save else "attend_back",
    )(qkv, dctx, lse, ids[:, None], ids[None, :], w_qkv, w_qkv, w_qkv, first, *behind)


def lefts_kernel(core_ref, *refs):
    sources, outs = refs[:8], refs[9:]
    rows = sources[0].shape[0]
    for n, out in enumerate(outs):
        own, other = sources[2 * n], sources[2 * n + 1]
        mine = own[0] if len(own.shape) == 3 else own[...]
        out[:, :rows] = mine.T
        out[:, rows:] = other[...].T


def lefts(core, pairs, act, act_other, behind):
    rows, width = pairs[0].shape
    steps = width // GROUP
    wide = act.shape[2] // steps
    tile = pl.BlockSpec((rows, GROUP), lambda i, c: (0, i))
    return pl.pallas_call(
        lefts_kernel,
        grid_spec=pltpu.PrefetchScalarGridSpec(
            num_scalar_prefetch=1,
            grid=(steps,),
            in_specs=[tile] * len(pairs) + [
                pl.BlockSpec((1, rows, wide), lambda i, c: (c[0], 0, i)),
                pl.BlockSpec((rows, wide), lambda i, c: (0, i)),
                pl.BlockSpec(memory_space=pl.ANY),
            ],
            out_specs=[pl.BlockSpec((GROUP, 2 * rows), lambda i, c: (i, 0))] * (len(pairs) // 2)
            + [pl.BlockSpec((wide, 2 * rows), lambda i, c: (i, 0))],
        ),
        out_shape=[jax.ShapeDtypeStruct((width, 2 * rows), BF16)] * (len(pairs) // 2)
        + [jax.ShapeDtypeStruct((act.shape[2], 2 * rows), BF16)],
        compiler_params=pltpu.CompilerParams(vmem_limit_bytes=VMEM_BYTES),
        cost_estimate=pl.CostEstimate(flops=int(10 * PEAK), bytes_accessed=0, transcendentals=0),
        name="lefts",
    )(core, *pairs, act, act_other, behind)


def grad_kernel(count, core_ref, *refs):
    extra_ref, out_ref = refs[3 * count:-1], refs[-1]
    at = 0
    for n in range(count):
        left, own, other = refs[3 * n:3 * n + 3]
        rows, cols = other.shape
        mine = own[0] if len(own.shape) == 3 else own[...]
        total = dot_nn(left[:, :rows], mine) + dot_nn(left[:, rows:], other[...])
        out_ref[:, at:at + cols] = total.astype(BF16)
        at += cols
    if extra_ref:
        out_ref[:, at:] = extra_ref[0][...]


def grad(core, parts, extra, name):
    size = min(512, GROUP * (parts[0][0].shape[0] // 768))
    height = parts[0][0].shape[0]
    in_specs, args, cols = [], [], 0
    for left, own, other in parts:
        rows, part = other.shape
        in_specs.append(pl.BlockSpec((size, left.shape[1]), lambda i, c: (i, 0)))
        if own.ndim == 3:
            in_specs.append(pl.BlockSpec((1, rows, part), lambda i, c: (c[0], 0, 0)))
        elif own.shape[1] == part:
            in_specs.append(pl.BlockSpec((rows, part), lambda i, c: (0, 0)))
        else:
            in_specs.append(pl.BlockSpec((rows, part), lambda i, c: (0, c[0])))
        in_specs.append(pl.BlockSpec((rows, part), lambda i, c: (0, 0)))
        args += [left, own, other]
        cols += part
    if extra is not None:
        in_specs.append(pl.BlockSpec((size, extra.shape[1]), lambda i, c: (i, 0)))
        args.append(extra)
        cols += extra.shape[1]
    return pl.pallas_call(
        functools.partial(grad_kernel, len(parts)),
        grid_spec=pltpu.PrefetchScalarGridSpec(
            num_scalar_prefetch=1,
            grid=(height // size,),
            in_specs=in_specs,
            out_specs=pl.BlockSpec((size, cols), lambda i, c: (i, 0)),
        ),
        out_shape=jax.ShapeDtypeStruct((height, cols), BF16),
        compiler_params=pltpu.CompilerParams(vmem_limit_bytes=VMEM_BYTES),
        cost_estimate=pl.CostEstimate(flops=int(1 * PEAK), bytes_accessed=0, transcendentals=0),
        name=name,
    )(core, *args)


def turned(block, axis, by):
    count = lax.axis_size(axis)
    return lax.ppermute(block, axis, [(i, (i + by) % count) for i in range(count)])


def around(block, axis):
    return [block] + [turned(block, axis, d) for d in range(1, lax.axis_size(axis))]


def place_kernel(plan, outs, at_ref, *refs):
    sources, out_refs, sems = refs[:len(plan)], refs[-1 - outs:-1], refs[-1]
    copies = []
    for n, (ref, (which, pick, where)) in enumerate(zip(sources, plan)):
        copies.append(pltpu.make_async_copy(pick(ref), where(out_refs[which], at_ref), sems.at[n]))
    for copy in copies:
        copy.start()
    for copy in copies:
        copy.wait()


def place(at, groups, name, behind=()):
    plan = [(n, pick, where) for n, (_, pieces) in enumerate(groups) for _, pick, where in pieces]
    arrays = [piece[0] for _, pieces in groups for piece in pieces]
    anywhere = pl.BlockSpec(memory_space=pl.ANY)
    return pl.pallas_call(
        functools.partial(place_kernel, plan, len(groups)),
        in_specs=[pl.BlockSpec(memory_space=pltpu.SMEM)] + [anywhere] * (len(arrays) + len(behind)),
        out_specs=[pl.BlockSpec(memory_space=pltpu.VMEM)] * len(groups),
        out_shape=[jax.ShapeDtypeStruct(shape, BF16) for shape, _ in groups],
        scratch_shapes=[pltpu.SemaphoreType.DMA((len(arrays),))],
        compiler_params=pltpu.CompilerParams(vmem_limit_bytes=VMEM_BYTES),
        cost_estimate=pl.CostEstimate(flops=int(5 * PEAK), bytes_accessed=0, transcendentals=0),
        name=name,
    )(at, *arrays, *behind)


X, Y, Z, C = range(4)


def after(block, other):
    return block + (other[(slice(0, 1),) * other.ndim].reshape(()) * 0).astype(block.dtype)


def spread(block, axis):
    count = lax.axis_size(axis)
    return lax.all_to_all(jnp.broadcast_to(block[None], (count,) + block.shape), axis, 0, 0, tiled=True)


def pieces_x(block):
    return [
        (part, lambda ref: ref, lambda out, at, e=e: out.at[:, (at[C] + e) % 2])
        for e, part in enumerate(around(block, "core"))
    ]


def pieces_around(blocks):
    return [
        (
            part,
            lambda ref: ref,
            lambda out, at, d=d, e=e: out.at[(at[X] + 4 - d) % 4, (at[C] + e) % 2],
        )
        for d, block in enumerate(blocks)
        for e, part in enumerate(around(block, "core"))
    ]


def pieces_xy(block):
    part = block.shape[2]
    return [
        (
            swapped,
            lambda ref, d=d: ref.at[d],
            lambda out, at, d=d, e=e, g=g: out.at[
                (at[X] + 4 - d) % 4, (at[C] + e) % 2, :,
                pl.ds(pl.multiple_of((at[Y] + 4 - g) % 4 * part, 128), part),
            ],
        )
        for g, moved in enumerate(around(block, "y"))
        for e, swapped in enumerate(around(moved, "core"))
        for d in range(4)
    ]


def pieces_xz(block):
    return [
        (
            swapped,
            lambda ref, d=d: ref.at[d],
            lambda out, at, d=d, e=e, g=g: out.at[
                (at[X] + 4 - d) % 4, (at[C] + e) % 2, (at[Z] + g) % 2
            ],
        )
        for g, moved in enumerate(around(block, "zl"))
        for e, swapped in enumerate(around(moved, "core"))
        for d in range(4)
    ]


def other_core(block):
    return lax.ppermute(block, "core", SWAP)


def other_half(block, behind=None):
    there = 1 - lax.axis_index("core")
    if block.ndim == 3:
        send = lax.dynamic_index_in_dim(block, there, 0, keepdims=False)
    else:
        half = block.shape[1] // 2
        send = lax.dynamic_slice_in_dim(block, there * half, half, 1)
    return other_core(send if behind is None else after(send, behind))


WIDE = ("fsdp", "zl", "y")


def exchange_sum(block):
    return jnp.sum(lax.all_to_all(block, WIDE, 0, 0, tiled=True).astype(F32), axis=0)


def emit_kernel(in_ref, down_ref, out_ref, g_in_ref, g_down_ref, g_out_ref):
    rows = g_in_ref.shape[0]
    g_in_ref[...] = in_ref[...].astype(F32).reshape(rows, -1)
    g_out_ref[...] = out_ref[...].astype(F32).reshape(rows, -1)
    pieces, _, rows, cols = down_ref.shape
    block = down_ref[...].astype(F32)
    for n in range(2 * pieces):
        at = (n % 2) * (cols // 2)
        g_down_ref[n * rows:(n + 1) * rows, :] = block[n // 2, 0, :, at:at + cols // 2]


def emit(early, width):
    pieces, cores, rows, _ = early.shape
    half, steps = width // 2, 2
    step = pieces // steps
    return pl.pallas_call(
        emit_kernel,
        grid=(steps, cores),
        in_specs=[
            pl.BlockSpec((step, 1, rows, 4 * half), lambda i, c: (i, c, 0, 0)),
            pl.BlockSpec((step, 1, rows, 4 * half), lambda i, c: (i, c, 0, 1)),
            pl.BlockSpec((step, 1, rows, half), lambda i, c: (i, c, 0, 8)),
        ],
        out_specs=[
            pl.BlockSpec((step * rows, 4 * half), lambda i, c: (i, c)),
            pl.BlockSpec((2 * step * rows, 2 * half), lambda i, c: (c * steps + i, 0)),
            pl.BlockSpec((step * rows, half), lambda i, c: (i, c)),
        ],
        out_shape=[
            jax.ShapeDtypeStruct((pieces * rows, 8 * half), F32),
            jax.ShapeDtypeStruct((2 * cores * pieces * rows, 2 * half), F32),
            jax.ShapeDtypeStruct((pieces * rows, 2 * half), F32),
        ],
        cost_estimate=pl.CostEstimate(flops=int(5 * PEAK), bytes_accessed=0, transcendentals=0),
        name="emit",
    )(early, early, early)


def joined(halves):
    return jnp.concatenate(halves, axis=-1).astype(F32)


def body(boundary, seq_ids, w_qkv, w_out, w_in, w_down, gains, biases, b_in):
    section = lax.axis_index("section")
    shard = lax.axis_index("fsdp")
    own = boundary[0, :, 0]
    micro, own_rows, width = own.shape
    shards = lax.axis_size("fsdp")
    rows = own_rows * shards
    hidden = b_in.shape[1] * shards
    piece = width // shards
    at = jnp.stack([lax.axis_index(name) for name in ("fsdp", "y", "zl", "core")]).astype(jnp.int32)

    small = jnp.concatenate([gains[0], biases[0], b_in[0].reshape(-1, piece)])
    small = jnp.pad(small.reshape(-1, width), ((0, 13), (0, 0)))
    padded = jnp.concatenate([own, jnp.zeros((shards - micro,) + own.shape[1:], BF16)])
    padded = jnp.concatenate([padded, jnp.broadcast_to(small[None], (shards,) + small.shape)], axis=1)

    half, part, cols = piece // 2, w_down.shape[1] // 4, w_in.shape[2] // 4
    own_in = lax.dynamic_slice(w_in[0], (at[C] * half, at[Y] * cols), (half, cols))
    own_down = lax.dynamic_slice_in_dim(w_down[0], (at[C] * 2 + at[Z]) * part, part, 0)
    own_out = lax.dynamic_slice_in_dim(w_out[0], at[C] * half, half, 0)
    own_qkv = lax.dynamic_slice_in_dim(w_qkv[0], at[C] * half, half, 0)
    in_blocks = around(own_in, "fsdp")
    down_blocks = around(after(own_down, in_blocks[1]), "fsdp")
    qkv_blocks = around(after(own_qkv, down_blocks[1]), "fsdp")
    padded = lax.all_to_all(padded, "fsdp", 0, 0, tiled=True)
    out_block = spread(after(own_out, qkv_blocks[1]), "fsdp")
    shape_x = (4, 2, half)
    (full_qkv,) = place(at, [(shape_x + (3 * width,), pieces_around(qkv_blocks))], "place_qkv")
    full_qkv = full_qkv.reshape(width, 3 * width)

    slot = padded[:, :own_rows].reshape(rows, width)
    small = padded[:, own_rows:own_rows + 3].reshape(shards, 12, piece)
    par = jnp.swapaxes(small[:, :8], 0, 1).reshape(8, width).astype(F32)
    bias_in = small[:, 8:].reshape(1, hidden).astype(F32)
    ids = lax.dynamic_index_in_dim(seq_ids[:, 0], jnp.minimum(shard, micro - 1), 0, keepdims=False)

    (ctx,) = attend(slot, full_qkv, par, ids, False)
    full_in, full_down, full_out = place(
        at,
        [
            (shape_x + (hidden,), pieces_xy(jnp.stack(in_blocks))),
            ((4, 2, 2, part, width), pieces_xz(jnp.stack(down_blocks))),
            (shape_x + (width,), pieces_x(out_block)),
        ],
        "place_rest",
        [ctx],
    )
    full_in = full_in.reshape(width, hidden)
    full_down = full_down.reshape(hidden, width)
    full_out = full_out.reshape(width, width)
    middle = feed(slot, ctx, full_out, full_in, full_down, par, bias_in, False)[0]
    arrived = lax.ppermute(middle, "section", [(0, 1)])

    h = jnp.where(section == 0, slot, arrived)
    ctx, qkv, lse = attend(h, full_qkv, par, ids, True)
    out, normed, xh1, inv1, xh2, inv2, slope, act = feed(
        h, ctx, full_out, full_in, full_down, par, bias_in, True
    )
    kept = (xh1, inv1, xh2, inv2, slope)

    cot = jnp.where(ids[:, None] >= 0, slot, jnp.zeros_like(slot))
    first, dctx = feed_back(cot, kept, full_out, full_in, full_down, par, False)
    (d_middle,) = attend_back(qkv, dctx, lse, ids, full_qkv, first, False)
    returned = lax.ppermute(d_middle, "section", [(1, 0)])

    core = at[C:]
    pairs = [part for block in (h, normed, ctx) for part in (block, other_core(block))]
    h2, normed2, ctx2, act2 = lefts(core, pairs, act, other_half(act), d_middle)

    g = jnp.where(section == 0, returned, cot)
    second, branch, sums2 = second_back(g, xh2, inv2, par, [h2, normed2, ctx2, act2])
    g_down = grad(core, [(act2, branch, other_core(branch))], None, "grad_down")
    s_down = exchange_sum(g_down.reshape(32, 48, width)).astype(BF16)
    first, dctx, inner, att, sums1, bin_sums = feed_back(
        second, (xh1, inv1, branch, inv2, slope), full_out, full_in, full_down, par, True, [g_down]
    )
    g_mid = grad(
        core, [(normed2, inner, other_half(inner)), (ctx2, att, other_half(att))], None, "grad_mid"
    )
    s_mid = exchange_sum(g_mid.reshape(32, 24, -1)).astype(BF16)
    d_h, dqkv, sums0 = attend_back(qkv, dctx, lse, ids, full_qkv, first, True, [g_mid, s_down])

    vec = (sums0 + sums1 + sums2).reshape(8, shards, piece)
    vec = jnp.concatenate([jnp.swapaxes(vec, 0, 1), bin_sums.reshape(shards, -1, piece)], axis=1)
    vec = jnp.pad(vec.reshape(shards, -1).astype(BF16), ((0, 0), (0, 768))).reshape(shards, 1, 24, 128)
    vec = jnp.broadcast_to(vec, (shards, 8, 24, 128)).reshape(768, 128)
    g_qkv = grad(core, [(h2, dqkv, other_half(dqkv))], vec, "grad_qkv").reshape(32, 24, -1)
    half = g_qkv.shape[2] - 128
    s_qkv = exchange_sum(g_qkv)

    wide = hidden // 2
    early = [s_mid[:, :wide], after(s_down[:24], g_qkv), s_down[24:], s_mid[:, wide:]]
    early = lax.all_gather(jnp.concatenate(early, axis=1), ("zl", "y", "core"))
    g_in, g_down, g_out = emit(early.reshape((8, 2) + early.shape[1:]), width)
    mine = spread(s_qkv[:, :half].astype(BF16), ("zl", "y"))
    other = lax.ppermute(mine, "core", SWAP)
    low = lax.axis_index("core") == 0
    g_qkv = joined([jnp.where(low, mine, other), jnp.where(low, other, mine)])
    vec = s_qkv[:, half:]
    vec = (vec + lax.ppermute(vec, "core", SWAP)).reshape(-1)[:12 * piece].reshape(12, piece)

    ends = jnp.where(section == 0, d_h, out).reshape(shards, own_rows, width)
    home = jnp.zeros_like(ends)
    for d in range(shards):
        block = lax.dynamic_index_in_dim(ends, (shard + d) % shards, 0)
        block = turned(block, "fsdp", d) if d else block
        home = lax.dynamic_update_slice_in_dim(home, block, (shard + shards - d) % shards, 0)
    ends = home[:micro].astype(F32)
    return (
        ends[None, :, None],
        g_qkv.reshape(1, 192, -1),
        g_out[None],
        g_in[None],
        g_down[None],
        vec[None, :2],
        vec[None, 2:8],
        vec[None, 8:].reshape(1, -1),
    )


def solution(mesh):
    fine = Mesh(mesh.devices.reshape(2, 4, 2, 4, 2), ("section", "fsdp", "zl", "y", "core"))
    dp = ("zl", "y", "core")
    in_specs = (
        P("section", None, None, dp + ("fsdp",), None),
        P(None, None, dp),
        P("section", "fsdp", None),
        P("section", "fsdp", None),
        P("section", "fsdp", None),
        P("section", "fsdp", None),
        P("section", None, "fsdp"),
        P("section", None, "fsdp"),
        P("section", "fsdp"),
    )
    out_specs = (
        P("section", None, None, dp + ("fsdp",), None),
        P("section", "fsdp", None),
        P("section", "fsdp", None),
        P("section", "fsdp", None),
        P("section", "fsdp", None),
        P("section", None, "fsdp"),
        P("section", None, "fsdp"),
        P("section", "fsdp"),
    )
    return jax.shard_map(body, mesh=fine, in_specs=in_specs, out_specs=out_specs, check_vma=False)
```

```python
import functools

import jax
import jax.numpy as jnp
from jax import lax
from jax.experimental import pallas as pl
from jax.experimental.pallas import tpu as pltpu
from jax.sharding import Mesh, PartitionSpec as P

HD = 64
GROUP = 256
TILE = 768
CHUNK = 64
EPS = 1e-06
PEAK = 1.1e9
SWAP = [(0, 1), (1, 0)]
F32 = jnp.float32
BF16 = jnp.bfloat16
VMEM_BYTES = 48 * 1024 * 1024


def dot_nn(a, b):
    return lax.dot_general(a, b, (((1,), (0,)), ((), ())), preferred_element_type=F32)


def dot_nt(a, b):
    return lax.dot_general(a, b, (((1,), (1,)), ((), ())), preferred_element_type=F32)


def dot_tn(a, b):
    return lax.dot_general(a, b, (((0,), (0,)), ((), ())), preferred_element_type=F32)


def chunks(rows, size=CHUNK):
    return [pl.ds(start, size) for start in range(0, rows, size)]


def attend_kernel(save, h_ref, wq_ref, wk_ref, wv_ref, par_ref, idc_ref, idr_ref, *rest):
    if save:
        ctx_ref, qkv_ref, lse_ref, mask_ref = rest
    else:
        ctx_ref, mask_ref = rest
    rows = h_ref.shape[0]

    @pl.when(pl.program_id(0) == 0)
    def _():
        for r in chunks(rows):
            mask_ref[r, :] = jnp.where(idc_ref[r, :] == idr_ref[...], 0.0, -1e30)

    h = h_ref[...]
    q = (dot_nn(h, wq_ref[...]) + par_ref[2:3, :]).astype(BF16)
    k = dot_nn(h, wk_ref[...]).astype(BF16)
    v = (dot_nn(h, wv_ref[...]) + par_ref[3:4, :]).astype(BF16)
    if save:
        qkv_ref[0] = q
        qkv_ref[1] = k
        qkv_ref[2] = v
    scaled = q * jnp.asarray(HD ** (-0.5), BF16)
    values_t = v.T
    parts = []
    for n in range(GROUP // HD):
        cols = slice(n * HD, (n + 1) * HD)
        st = dot_nt(k[:, cols], scaled[:, cols]) + mask_ref[...]
        top = jnp.max(st, axis=0, keepdims=True)
        e = jnp.exp(st - top)
        total = jnp.sum(e, axis=0, keepdims=True)
        parts.append(dot_nn(values_t[cols, :], e.astype(BF16)) * (1.0 / total))
        if save:
            lse_ref[n:n + 1, :] = top + jnp.log(total)
    ctx_ref[...] = jnp.concatenate(parts, axis=0).T.astype(BF16)


def attend(h, w_qkv, par, ids, save):
    rows, width = h.shape
    steps = width // GROUP
    out_shape = [jax.ShapeDtypeStruct((rows, width), BF16)]
    out_specs = [pl.BlockSpec((rows, GROUP), lambda j: (0, j))]
    if save:
        out_shape += [
            jax.ShapeDtypeStruct((3, rows, width), BF16),
            jax.ShapeDtypeStruct((8 * steps, rows), F32),
        ]
        out_specs += [
            pl.BlockSpec((3, rows, GROUP), lambda j: (0, 0, j)),
            pl.BlockSpec((8, rows), lambda j: (j, 0)),
        ]
    return pl.pallas_call(
        functools.partial(attend_kernel, save),
        grid=(steps,),
        in_specs=[
            pl.BlockSpec((rows, width), lambda j: (0, 0)),
            pl.BlockSpec((width, GROUP), lambda j: (0, j)),
            pl.BlockSpec((width, GROUP), lambda j: (0, j + steps)),
            pl.BlockSpec((width, GROUP), lambda j: (0, j + 2 * steps)),
            pl.BlockSpec((8, GROUP), lambda j: (0, j)),
            pl.BlockSpec((rows, 1), lambda j: (0, 0)),
            pl.BlockSpec((1, rows), lambda j: (0, 0)),
        ],
        out_specs=out_specs,
        out_shape=out_shape,
        scratch_shapes=[pltpu.VMEM((rows, rows), F32)],
        compiler_params=pltpu.CompilerParams(vmem_limit_bytes=VMEM_BYTES),
        cost_estimate=pl.CostEstimate(flops=int(10 * PEAK), bytes_accessed=0, transcendentals=0),
        name="attend_save" if save else "attend",
    )(h, w_qkv, w_qkv, w_qkv, par, ids[:, None], ids[None, :])


def normalise(u):
    center = u - jnp.mean(u, axis=-1, keepdims=True)
    inv = lax.rsqrt(jnp.mean(center * center, axis=-1, keepdims=True) + EPS)
    return center * inv, inv


def feed_kernel(save, h_ref, ctx_ref, wo_ref, wi_ref, wd_ref, par_ref, bi_ref, *rest):
    if save:
        (out_ref, normed_ref, xh1_ref, inv1_ref, xh2_ref, inv2_ref, slope_ref, kept_ref,
         acc_ref, inner_ref, act_ref) = rest
    else:
        out_ref, normed_ref, acc_ref, inner_ref, act_ref = rest
    rows = h_ref.shape[0]
    step = pl.program_id(0)

    @pl.when(step == 0)
    def _():
        acc_ref[...] = dot_nn(ctx_ref[...], wo_ref[...])
        for r in chunks(rows):
            first = h_ref[r, :].astype(F32) + (acc_ref[r, :] + par_ref[4:5, :])
            xh, inv = normalise(first)
            normed = (xh * par_ref[0:1, :] + par_ref[5:6, :]).astype(BF16)
            normed_ref[r, :] = normed
            acc_ref[r, :] = normed.astype(F32) + par_ref[6:7, :]
            if save:
                xh1_ref[r, :] = xh
                inv1_ref[r, :] = inv

    inner_ref[...] = dot_nn(normed_ref[...], wi_ref[...])
    for r in chunks(rows):
        t = inner_ref[r, :] + bi_ref[...]
        half = 0.5 * lax.erf(t * 0.7071067811865476) + 0.5
        act = (t * half).astype(BF16)
        act_ref[r, :] = act
        if save:
            kept_ref[0, r, :] = act[:, :TILE // 2]
            kept_ref[1, r, :] = act[:, TILE // 2:]
            bell = jnp.exp(-0.5 * (t * t)) * 0.3989422804014327
            slope_ref[r, :] = (half + t * bell).astype(BF16)
    acc_ref[...] += dot_nn(act_ref[...], wd_ref[...])

    @pl.when(step == pl.num_programs(0) - 1)
    def _():
        for r in chunks(rows):
            xh, inv = normalise(acc_ref[r, :])
            out_ref[r, :] = (xh * par_ref[1:2, :] + par_ref[7:8, :]).astype(BF16)
            if save:
                xh2_ref[r, :] = xh
                inv2_ref[r, :] = inv


def feed(h, ctx, w_out, w_in, w_down, par, b_in, save):
    rows, width = h.shape
    hidden = w_in.shape[1]
    steps = hidden // TILE
    whole = lambda j: (0, 0)
    out_shape = [
        jax.ShapeDtypeStruct((rows, width), BF16),
        jax.ShapeDtypeStruct((rows, width), BF16),
    ]
    out_specs = [pl.BlockSpec((rows, width), whole), pl.BlockSpec((rows, width), whole)]
    scratch = [pltpu.VMEM((rows, width), F32), pltpu.VMEM((rows, TILE), F32)]
    if save:
        for shape in ((rows, width), (rows, 1), (rows, width), (rows, 1)):
            out_shape.append(jax.ShapeDtypeStruct(shape, F32))
            out_specs.append(pl.BlockSpec(shape, whole))
        out_shape.append(jax.ShapeDtypeStruct((rows, hidden), BF16))
        out_specs.append(pl.BlockSpec((rows, TILE), lambda j: (0, j)))
        out_shape.append(jax.ShapeDtypeStruct((2, rows, hidden // 2), BF16))
        out_specs.append(pl.BlockSpec((2, rows, TILE // 2), lambda j: (0, 0, j)))
    scratch.append(pltpu.VMEM((rows, TILE), BF16))
    return pl.pallas_call(
        functools.partial(feed_kernel, save),
        grid=(steps,),
        in_specs=[
            pl.BlockSpec((rows, width), whole),
            pl.BlockSpec((rows, width), whole),
            pl.BlockSpec((width, width), whole),
            pl.BlockSpec((width, TILE), lambda j: (0, j)),
            pl.BlockSpec((TILE, width), lambda j: (j, 0)),
            pl.BlockSpec((8, width), whole),
            pl.BlockSpec((1, TILE), lambda j: (0, j)),
        ],
        out_specs=out_specs,
        out_shape=out_shape,
        scratch_shapes=scratch,
        compiler_params=pltpu.CompilerParams(vmem_limit_bytes=VMEM_BYTES),
        cost_estimate=pl.CostEstimate(flops=int((15 if save else 12) * PEAK), bytes_accessed=0, transcendentals=0),
        name="feed_save" if save else "feed",
    )(h, ctx, w_out, w_in, w_down, par, b_in)


def norm_back(g, xh, inv, gain):
    weighted = g * gain
    mean = jnp.mean(weighted, axis=-1, keepdims=True)
    slope = jnp.mean(weighted * xh, axis=-1, keepdims=True)
    return (weighted - mean - xh * slope) * inv


def col_sum(rows):
    return jnp.sum(rows, axis=0, keepdims=True)


def norm_back_kernel(g_ref, xh_ref, inv_ref, par_ref, *rest):
    second_ref, branch_ref, sums_ref = rest[-3:]
    rows, width = g_ref.shape
    gain_sum = shift_sum = branch_sum = jnp.zeros((1, width), F32)
    for r in chunks(rows):
        g = g_ref[r, :].astype(F32)
        xh = xh_ref[r, :]
        second = norm_back(g, xh, inv_ref[r, :], par_ref[1:2, :])
        second_ref[r, :] = second
        branch = second.astype(BF16)
        branch_ref[r, :] = branch
        gain_sum += col_sum(g * xh)
        shift_sum += col_sum(g)
        branch_sum += col_sum(branch.astype(F32))
    sums_ref[...] = jnp.zeros_like(sums_ref)
    sums_ref[1:2, :] = gain_sum
    sums_ref[7:8, :] = shift_sum
    sums_ref[6:7, :] = branch_sum


def second_back(g, xh, inv, par, behind):
    rows, width = xh.shape
    vmem = pl.BlockSpec(memory_space=pltpu.VMEM)
    return pl.pallas_call(
        norm_back_kernel,
        in_specs=[vmem] * 4 + [pl.BlockSpec(memory_space=pl.ANY)] * len(behind),
        out_specs=[vmem] * 3,
        out_shape=[
            jax.ShapeDtypeStruct((rows, width), F32),
            jax.ShapeDtypeStruct((rows, width), BF16),
            jax.ShapeDtypeStruct((8, width), F32),
        ],
        compiler_params=pltpu.CompilerParams(vmem_limit_bytes=VMEM_BYTES),
        cost_estimate=pl.CostEstimate(flops=int(3 * PEAK), bytes_accessed=0, transcendentals=0),
        name="second_back",
    )(g, xh, inv, par, *behind)


def feed_back_kernel(save, g_ref, xh2_ref, inv2_ref, xh1_ref, inv1_ref, slope_ref, wd_ref, wi_ref, wo_ref,
                     par_ref, *rest):
    if save:
        first_ref, dctx_ref, inner_ref, att_ref, sums_ref, bsum_ref, acc_ref, dact_ref = rest[1:]
        branch_ref = xh2_ref
    else:
        first_ref, dctx_ref, acc_ref, dact_ref, branch_ref, inner_ref, att_ref = rest
    rows, width = g_ref.shape
    step = pl.program_id(0)

    @pl.when(step == 0)
    def _():
        if save:
            acc_ref[...] = g_ref[...]
            sums_ref[...] = jnp.zeros_like(sums_ref)
        else:
            for r in chunks(rows):
                g = g_ref[r, :].astype(F32)
                second = norm_back(g, xh2_ref[r, :], inv2_ref[r, :], par_ref[1:2, :])
                acc_ref[r, :] = second
                branch_ref[r, :] = second.astype(BF16)

    dact_ref[...] = dot_nt(branch_ref[...], wd_ref[...])
    bin_sum = jnp.zeros((1, dact_ref.shape[1]), F32)
    for r in chunks(rows):
        inner = (dact_ref[r, :] * slope_ref[r, :].astype(F32)).astype(BF16)
        if save:
            inner_ref[0, r, :] = inner
        else:
            inner_ref[r, :] = inner
        if save:
            bin_sum += col_sum(inner.astype(F32))
    if save:
        bsum_ref[...] = bin_sum
    acc_ref[...] += dot_nt(inner_ref[0] if save else inner_ref[...], wi_ref[...])

    @pl.when(step == pl.num_programs(0) - 1)
    def _():
        gain_sum = shift_sum = att_sum = jnp.zeros((1, width), F32)
        for r in chunks(rows):
            g = acc_ref[r, :]
            xh = xh1_ref[r, :]
            first = norm_back(g, xh, inv1_ref[r, :], par_ref[0:1, :])
            first_ref[r, :] = first
            att = first.astype(BF16)
            att_ref[r, :] = att
            if save:
                gain_sum += col_sum(g * xh)
                shift_sum += col_sum(g)
                att_sum += col_sum(att.astype(F32))
        if save:
            sums_ref[0:1, :] = gain_sum
            sums_ref[5:6, :] = shift_sum
            sums_ref[4:5, :] = att_sum
        dctx_ref[...] = dot_nt(att_ref[...], wo_ref[...]).astype(BF16)


def feed_back(g, kept, w_out, w_in, w_down, par, save, behind=()):
    xh1, inv1, xh2, inv2, slope = kept
    rows, width = xh1.shape
    hidden = slope.shape[1]
    steps = hidden // TILE
    whole = lambda j: (0, 0)
    full = pl.BlockSpec((rows, width), whole)
    tile = pl.BlockSpec((rows, TILE), lambda j: (0, j))
    out_shape = [jax.ShapeDtypeStruct((rows, width), F32), jax.ShapeDtypeStruct((rows, width), BF16)]
    out_specs = [full, full]
    scratch = [pltpu.VMEM((rows, width), F32), pltpu.VMEM((rows, TILE), F32)]
    if save:
        out_shape += [
            jax.ShapeDtypeStruct((2, rows, hidden // 2), BF16),
            jax.ShapeDtypeStruct((rows, width), BF16),
            jax.ShapeDtypeStruct((8, width), F32),
            jax.ShapeDtypeStruct((1, hidden), F32),
        ]
        out_specs += [
            pl.BlockSpec((1, rows, TILE), lambda j: (j // (steps // 2), 0, j % (steps // 2))), full,
            pl.BlockSpec((8, width), whole),
            pl.BlockSpec((1, TILE), lambda j: (0, j)),
        ]
    else:
        scratch += [pltpu.VMEM((rows, width), BF16), pltpu.VMEM((rows, TILE), BF16), pltpu.VMEM((rows, width), BF16)]
    return pl.pallas_call(
        functools.partial(feed_back_kernel, save),
        grid=(steps,),
        in_specs=[
            full, full, pl.BlockSpec((rows, 1), whole), full, pl.BlockSpec((rows, 1), whole), tile,
            pl.BlockSpec((TILE, width), lambda j: (j, 0)),
            pl.BlockSpec((width, TILE), lambda j: (0, j)),
            pl.BlockSpec((width, width), whole),
            pl.BlockSpec((8, width), whole),
        ] + [pl.BlockSpec(memory_space=pl.ANY)] * len(behind),
        out_specs=out_specs,
        out_shape=out_shape,
        scratch_shapes=scratch,
        compiler_params=pltpu.CompilerParams(vmem_limit_bytes=VMEM_BYTES),
        cost_estimate=pl.CostEstimate(flops=int((15 if save else 12) * PEAK), bytes_accessed=0, transcendentals=0),
        name="feed_back_save" if save else "feed_back",
    )(g, xh2, inv2, xh1, inv1, slope, w_down, w_in, w_out, par, *behind)


def attend_back_kernel(save, qkv_ref, dctx_ref, lse_ref, idc_ref, idr_ref, wq_ref, wk_ref, wv_ref, first_ref, *rest):
    if save:
        dh_ref, dqkv_ref, sums_ref, mask_ref, acc_ref = rest[-5:]
    else:
        dh_ref, mask_ref, acc_ref = rest
    rows = first_ref.shape[0]
    step = pl.program_id(0)

    @pl.when(step == 0)
    def _():
        for r in chunks(rows):
            mask_ref[r, :] = jnp.where(idc_ref[r, :] == idr_ref[...], 0.0, -1e30)
        acc_ref[...] = first_ref[...]

    scale = HD ** (-0.5)
    q = qkv_ref[0] * jnp.asarray(scale, BF16)
    k = qkv_ref[1]
    v = qkv_ref[2]
    dctx = dctx_ref[...]
    keys_t = k.T
    dq_t = []
    dk = []
    dv = []
    for n in range(GROUP // HD):
        cols = slice(n * HD, (n + 1) * HD)
        lse = lse_ref[n:n + 1, :]
        st = dot_nt(k[:, cols], q[:, cols]) + mask_ref[...]
        pt = jnp.exp(st - lse)
        dpt = dot_nt(v[:, cols], dctx[:, cols])
        row = jnp.sum(pt * dpt, axis=0, keepdims=True)
        dst = (pt * (dpt - row)).astype(BF16)
        dv.append(dot_nn(pt.astype(BF16), dctx[:, cols]))
        dk.append(dot_nn(dst, q[:, cols]))
        dq_t.append(dot_nn(keys_t[cols, :], dst))
    dq = (jnp.concatenate(dq_t, axis=0).T * scale).astype(BF16)
    dk = jnp.concatenate(dk, axis=1).astype(BF16)
    dv = jnp.concatenate(dv, axis=1).astype(BF16)
    if save:
        for n, part in enumerate((dq, dk, dv)):
            offset = n * first_ref.shape[1] + step * GROUP
            dqkv_ref[:, pl.ds(pl.multiple_of(offset, GROUP), GROUP)] = part
        sums_ref[...] = jnp.zeros_like(sums_ref)
        sums_ref[2:3, :] = col_sum(dq.astype(F32))
        sums_ref[3:4, :] = col_sum(dv.astype(F32))
    acc_ref[...] += dot_nt(dq, wq_ref[...]) + dot_nt(dk, wk_ref[...]) + dot_nt(dv, wv_ref[...])

    @pl.when(step == pl.num_programs(0) - 1)
    def _():
        dh_ref[...] = acc_ref[...].astype(BF16)


def attend_back(qkv, dctx, lse, ids, w_qkv, first, save, behind=()):
    rows, width = first.shape
    steps = width // GROUP
    whole = lambda j: (0, 0)
    full = pl.BlockSpec((rows, width), whole)
    out_shape = [jax.ShapeDtypeStruct((rows, width), BF16)]
    out_specs = [full]
    if save:
        out_shape += [jax.ShapeDtypeStruct((rows, 3 * width), BF16), jax.ShapeDtypeStruct((8, width), F32)]
        out_specs += [
            pl.BlockSpec((rows, 3 * width), whole),
            pl.BlockSpec((8, GROUP), lambda j: (0, j)),
        ]
    return pl.pallas_call(
        functools.partial(attend_back_kernel, save),
        grid=(steps,),
        in_specs=[
            pl.BlockSpec((3, rows, GROUP), lambda j: (0, 0, j)),
            pl.BlockSpec((rows, GROUP), lambda j: (0, j)),
            pl.BlockSpec((8, rows), lambda j: (j, 0)),
            pl.BlockSpec((rows, 1), whole),
            pl.BlockSpec((1, rows), whole),
            pl.BlockSpec((width, GROUP), lambda j: (0, j)),
            pl.BlockSpec((width, GROUP), lambda j: (0, j + steps)),
            pl.BlockSpec((width, GROUP), lambda j: (0, j + 2 * steps)),
            full,
        ] + [pl.BlockSpec(memory_space=pl.ANY)] * len(behind),
        out_specs=out_specs,
        out_shape=out_shape,
        scratch_shapes=[pltpu.VMEM((rows, rows), F32), pltpu.VMEM((rows, width), F32)],
        compiler_params=pltpu.CompilerParams(vmem_limit_bytes=VMEM_BYTES),
        cost_estimate=pl.CostEstimate(flops=int(14 * PEAK), bytes_accessed=0, transcendentals=0),
        name="attend_back_save" if save else "attend_back",
    )(qkv, dctx, lse, ids[:, None], ids[None, :], w_qkv, w_qkv, w_qkv, first, *behind)


def lefts_kernel(core_ref, *refs):
    sources, outs = refs[:8], refs[9:]
    rows = sources[0].shape[0]
    for n, out in enumerate(outs):
        own, other = sources[2 * n], sources[2 * n + 1]
        mine = own[0] if len(own.shape) == 3 else own[...]
        out[:, :rows] = mine.T
        out[:, rows:] = other[...].T


def lefts(core, pairs, act, act_other, behind):
    rows, width = pairs[0].shape
    steps = width // GROUP
    wide = act.shape[2] // steps
    tile = pl.BlockSpec((rows, GROUP), lambda i, c: (0, i))
    return pl.pallas_call(
        lefts_kernel,
        grid_spec=pltpu.PrefetchScalarGridSpec(
            num_scalar_prefetch=1,
            grid=(steps,),
            in_specs=[tile] * len(pairs) + [
                pl.BlockSpec((1, rows, wide), lambda i, c: (c[0], 0, i)),
                pl.BlockSpec((rows, wide), lambda i, c: (0, i)),
                pl.BlockSpec(memory_space=pl.ANY),
            ],
            out_specs=[pl.BlockSpec((GROUP, 2 * rows), lambda i, c: (i, 0))] * (len(pairs) // 2)
            + [pl.BlockSpec((wide, 2 * rows), lambda i, c: (i, 0))],
        ),
        out_shape=[jax.ShapeDtypeStruct((width, 2 * rows), BF16)] * (len(pairs) // 2)
        + [jax.ShapeDtypeStruct((act.shape[2], 2 * rows), BF16)],
        compiler_params=pltpu.CompilerParams(vmem_limit_bytes=VMEM_BYTES),
        cost_estimate=pl.CostEstimate(flops=int(10 * PEAK), bytes_accessed=0, transcendentals=0),
        name="lefts",
    )(core, *pairs, act, act_other, behind)


def grad_kernel(count, core_ref, *refs):
    extra_ref, out_ref = refs[3 * count:-1], refs[-1]
    at = 0
    for n in range(count):
        left, own, other = refs[3 * n:3 * n + 3]
        rows, cols = other.shape
        mine = own[0] if len(own.shape) == 3 else own[...]
        total = dot_nn(left[:, :rows], mine) + dot_nn(left[:, rows:], other[...])
        out_ref[:, at:at + cols] = total.astype(BF16)
        at += cols
    if extra_ref:
        out_ref[:, at:] = extra_ref[0][...]


def grad(core, parts, extra, name):
    size = min(512, GROUP * (parts[0][0].shape[0] // 768))
    height = parts[0][0].shape[0]
    in_specs, args, cols = [], [], 0
    for left, own, other in parts:
        rows, part = other.shape
        in_specs.append(pl.BlockSpec((size, left.shape[1]), lambda i, c: (i, 0)))
        if own.ndim == 3:
            in_specs.append(pl.BlockSpec((1, rows, part), lambda i, c: (c[0], 0, 0)))
        elif own.shape[1] == part:
            in_specs.append(pl.BlockSpec((rows, part), lambda i, c: (0, 0)))
        else:
            in_specs.append(pl.BlockSpec((rows, part), lambda i, c: (0, c[0])))
        in_specs.append(pl.BlockSpec((rows, part), lambda i, c: (0, 0)))
        args += [left, own, other]
        cols += part
    if extra is not None:
        in_specs.append(pl.BlockSpec((size, extra.shape[1]), lambda i, c: (i, 0)))
        args.append(extra)
        cols += extra.shape[1]
    return pl.pallas_call(
        functools.partial(grad_kernel, len(parts)),
        grid_spec=pltpu.PrefetchScalarGridSpec(
            num_scalar_prefetch=1,
            grid=(height // size,),
            in_specs=in_specs,
            out_specs=pl.BlockSpec((size, cols), lambda i, c: (i, 0)),
        ),
        out_shape=jax.ShapeDtypeStruct((height, cols), BF16),
        compiler_params=pltpu.CompilerParams(vmem_limit_bytes=VMEM_BYTES),
        cost_estimate=pl.CostEstimate(flops=int(1 * PEAK), bytes_accessed=0, transcendentals=0),
        name=name,
    )(core, *args)


def turned(block, axis, by):
    count = lax.axis_size(axis)
    return lax.ppermute(block, axis, [(i, (i + by) % count) for i in range(count)])


def around(block, axis):
    return [block] + [turned(block, axis, d) for d in range(1, lax.axis_size(axis))]


def place_kernel(plan, outs, at_ref, *refs):
    sources, out_refs, sems = refs[:len(plan)], refs[-1 - outs:-1], refs[-1]
    copies = []
    for n, (ref, (which, pick, where)) in enumerate(zip(sources, plan)):
        copies.append(pltpu.make_async_copy(pick(ref), where(out_refs[which], at_ref), sems.at[n]))
    for copy in copies:
        copy.start()
    for copy in copies:
        copy.wait()


def place(at, groups, name, behind=()):
    plan = [(n, pick, where) for n, (_, pieces) in enumerate(groups) for _, pick, where in pieces]
    arrays = [piece[0] for _, pieces in groups for piece in pieces]
    anywhere = pl.BlockSpec(memory_space=pl.ANY)
    return pl.pallas_call(
        functools.partial(place_kernel, plan, len(groups)),
        in_specs=[pl.BlockSpec(memory_space=pltpu.SMEM)] + [anywhere] * (len(arrays) + len(behind)),
        out_specs=[pl.BlockSpec(memory_space=pltpu.VMEM)] * len(groups),
        out_shape=[jax.ShapeDtypeStruct(shape, BF16) for shape, _ in groups],
        scratch_shapes=[pltpu.SemaphoreType.DMA((len(arrays),))],
        compiler_params=pltpu.CompilerParams(vmem_limit_bytes=VMEM_BYTES),
        cost_estimate=pl.CostEstimate(flops=int(5 * PEAK), bytes_accessed=0, transcendentals=0),
        name=name,
    )(at, *arrays, *behind)


X, Y, Z, C = range(4)


def after(block, other):
    return block + (other[(slice(0, 1),) * other.ndim].reshape(()) * 0).astype(block.dtype)


def spread(block, axis):
    count = lax.axis_size(axis)
    return lax.all_to_all(jnp.broadcast_to(block[None], (count,) + block.shape), axis, 0, 0, tiled=True)


def pieces_x(block):
    return [
        (
            part,
            lambda ref, d=d: ref.at[d],
            lambda out, at, d=d, e=e: out.at[(at[X] + 4 - d) % 4, (at[C] + e) % 2],
        )
        for e, part in enumerate(around(block, "core"))
        for d in range(4)
    ]


def pieces_around(blocks):
    return [
        (
            part,
            lambda ref: ref,
            lambda out, at, d=d, e=e: out.at[(at[X] + 4 - d) % 4, (at[C] + e) % 2],
        )
        for d, block in enumerate(blocks)
        for e, part in enumerate(around(block, "core"))
    ]


def pieces_xy(block):
    part = block.shape[2]
    return [
        (
            swapped,
            lambda ref, d=d: ref.at[d],
            lambda out, at, d=d, e=e, g=g: out.at[
                (at[X] + 4 - d) % 4, (at[C] + e) % 2, :,
                pl.ds(pl.multiple_of((at[Y] + 4 - g) % 4 * part, 128), part),
            ],
        )
        for g, moved in enumerate(around(block, "y"))
        for e, swapped in enumerate(around(moved, "core"))
        for d in range(4)
    ]


def pieces_xz(block):
    return [
        (
            swapped,
            lambda ref, d=d: ref.at[d],
            lambda out, at, d=d, e=e, g=g: out.at[
                (at[X] + 4 - d) % 4, (at[C] + e) % 2, (at[Z] + g) % 2
            ],
        )
        for g, moved in enumerate(around(block, "zl"))
        for e, swapped in enumerate(around(moved, "core"))
        for d in range(4)
    ]


def other_core(block):
    return lax.ppermute(block, "core", SWAP)


def other_half(block, behind=None):
    there = 1 - lax.axis_index("core")
    if block.ndim == 3:
        send = lax.dynamic_index_in_dim(block, there, 0, keepdims=False)
    else:
        half = block.shape[1] // 2
        send = lax.dynamic_slice_in_dim(block, there * half, half, 1)
    return other_core(send if behind is None else after(send, behind))


WIDE = ("fsdp", "zl", "y")


def exchange_sum(block):
    return jnp.sum(lax.all_to_all(block, WIDE, 0, 0, tiled=True).astype(F32), axis=0)


def emit_kernel(in_ref, down_ref, out_ref, g_in_ref, g_down_ref, g_out_ref):
    rows = g_in_ref.shape[0]
    g_in_ref[...] = in_ref[...].astype(F32).reshape(rows, -1)
    g_out_ref[...] = out_ref[...].astype(F32).reshape(rows, -1)
    pieces, _, rows, cols = down_ref.shape
    block = down_ref[...].astype(F32)
    for n in range(2 * pieces):
        at = (n % 2) * (cols // 2)
        g_down_ref[n * rows:(n + 1) * rows, :] = block[n // 2, 0, :, at:at + cols // 2]


def emit(early, width):
    pieces, cores, rows, _ = early.shape
    half, steps = width // 2, 2
    step = pieces // steps
    return pl.pallas_call(
        emit_kernel,
        grid=(steps, cores),
        in_specs=[
            pl.BlockSpec((step, 1, rows, 4 * half), lambda i, c: (i, c, 0, 0)),
            pl.BlockSpec((step, 1, rows, 4 * half), lambda i, c: (i, c, 0, 1)),
            pl.BlockSpec((step, 1, rows, half), lambda i, c: (i, c, 0, 8)),
        ],
        out_specs=[
            pl.BlockSpec((step * rows, 4 * half), lambda i, c: (i, c)),
            pl.BlockSpec((2 * step * rows, 2 * half), lambda i, c: (c * steps + i, 0)),
            pl.BlockSpec((step * rows, half), lambda i, c: (i, c)),
        ],
        out_shape=[
            jax.ShapeDtypeStruct((pieces * rows, 8 * half), F32),
            jax.ShapeDtypeStruct((2 * cores * pieces * rows, 2 * half), F32),
            jax.ShapeDtypeStruct((pieces * rows, 2 * half), F32),
        ],
        cost_estimate=pl.CostEstimate(flops=int(5 * PEAK), bytes_accessed=0, transcendentals=0),
        name="emit",
    )(early, early, early)


def joined(halves):
    return jnp.concatenate(halves, axis=-1).astype(F32)


def body(boundary, seq_ids, w_qkv, w_out, w_in, w_down, gains, biases, b_in):
    section = lax.axis_index("section")
    shard = lax.axis_index("fsdp")
    own = boundary[0, :, 0]
    micro, own_rows, width = own.shape
    shards = lax.axis_size("fsdp")
    rows = own_rows * shards
    hidden = b_in.shape[1] * shards
    piece = width // shards
    at = jnp.stack([lax.axis_index(name) for name in ("fsdp", "y", "zl", "core")]).astype(jnp.int32)

    small = jnp.concatenate([gains[0], biases[0], b_in[0].reshape(-1, piece)])
    small = jnp.pad(small.reshape(-1, width), ((0, 13), (0, 0)))
    padded = jnp.concatenate([own, jnp.zeros((shards - micro,) + own.shape[1:], BF16)])
    padded = jnp.concatenate([padded, jnp.broadcast_to(small[None], (shards,) + small.shape)], axis=1)

    half, part, cols = piece // 2, w_down.shape[1] // 4, w_in.shape[2] // 4
    own_in = lax.dynamic_slice(w_in[0], (at[C] * half, at[Y] * cols), (half, cols))
    own_down = lax.dynamic_slice_in_dim(w_down[0], (at[C] * 2 + at[Z]) * part, part, 0)
    own_out = lax.dynamic_slice_in_dim(w_out[0], at[C] * half, half, 0)
    own_qkv = lax.dynamic_slice_in_dim(w_qkv[0], at[C] * half, half, 0)
    in_blocks = around(jnp.concatenate([own_in, own_out]), "fsdp")
    down_blocks = around(after(own_down, in_blocks[1]), "fsdp")
    qkv_blocks = around(after(own_qkv, down_blocks[1]), "fsdp")
    padded = lax.all_to_all(padded, "fsdp", 0, 0, tiled=True)
    in_block = jnp.stack([block[:half] for block in in_blocks])
    out_block = jnp.stack([block[half:] for block in in_blocks])
    shape_x = (4, 2, half)
    (full_qkv,) = place(at, [(shape_x + (3 * width,), pieces_around(qkv_blocks))], "place_qkv")
    full_qkv = full_qkv.reshape(width, 3 * width)

    slot = padded[:, :own_rows].reshape(rows, width)
    small = padded[:, own_rows:own_rows + 3].reshape(shards, 12, piece)
    par = jnp.swapaxes(small[:, :8], 0, 1).reshape(8, width).astype(F32)
    bias_in = small[:, 8:].reshape(1, hidden).astype(F32)
    ids = lax.dynamic_index_in_dim(seq_ids[:, 0], jnp.minimum(shard, micro - 1), 0, keepdims=False)

    (ctx,) = attend(slot, full_qkv, par, ids, False)
    full_in, full_down, full_out = place(
        at,
        [
            (shape_x + (hidden,), pieces_xy(in_block)),
            ((4, 2, 2, part, width), pieces_xz(jnp.stack(down_blocks))),
            (shape_x + (width,), pieces_x(out_block)),
        ],
        "place_rest",
        [ctx],
    )
    full_in = full_in.reshape(width, hidden)
    full_down = full_down.reshape(hidden, width)
    full_out = full_out.reshape(width, width)
    middle = feed(slot, ctx, full_out, full_in, full_down, par, bias_in, False)[0]
    arrived = lax.ppermute(middle, "section", [(0, 1)])

    h = jnp.where(section == 0, slot, arrived)
    ctx, qkv, lse = attend(h, full_qkv, par, ids, True)
    out, normed, xh1, inv1, xh2, inv2, slope, act = feed(
        h, ctx, full_out, full_in, full_down, par, bias_in, True
    )
    kept = (xh1, inv1, xh2, inv2, slope)

    cot = jnp.where(ids[:, None] >= 0, slot, jnp.zeros_like(slot))
    first, dctx = feed_back(cot, kept, full_out, full_in, full_down, par, False)
    (d_middle,) = attend_back(qkv, dctx, lse, ids, full_qkv, first, False)
    returned = lax.ppermute(d_middle, "section", [(1, 0)])

    core = at[C:]
    pairs = [part for block in (h, normed, ctx) for part in (block, other_core(block))]
    h2, normed2, ctx2, act2 = lefts(core, pairs, act, other_half(act), d_middle)

    g = jnp.where(section == 0, returned, after(cot, h2))
    second, branch, sums2 = second_back(g, xh2, inv2, par, [h2, normed2, ctx2, act2])
    g_down = grad(core, [(act2, branch, other_core(branch))], None, "grad_down")
    s_down = exchange_sum(g_down.reshape(32, 48, width)).astype(BF16)
    first, dctx, inner, att, sums1, bin_sums = feed_back(
        second, (xh1, inv1, branch, inv2, slope), full_out, full_in, full_down, par, True, [g_down]
    )
    g_mid = grad(
        core, [(normed2, inner, other_half(inner)), (ctx2, att, other_half(att))], None, "grad_mid"
    )
    s_mid = exchange_sum(g_mid.reshape(32, 24, -1)).astype(BF16)
    d_h, dqkv, sums0 = attend_back(qkv, dctx, lse, ids, full_qkv, first, True, [g_mid, s_down])

    vec = (sums0 + sums1 + sums2).reshape(8, shards, piece)
    vec = jnp.concatenate([jnp.swapaxes(vec, 0, 1), bin_sums.reshape(shards, -1, piece)], axis=1)
    vec = jnp.pad(vec.reshape(shards, -1).astype(BF16), ((0, 0), (0, 768))).reshape(shards, 1, 24, 128)
    vec = jnp.broadcast_to(vec, (shards, 8, 24, 128)).reshape(768, 128)
    g_qkv = grad(core, [(h2, dqkv, other_half(dqkv))], vec, "grad_qkv").reshape(32, 24, -1)
    half = g_qkv.shape[2] - 128
    s_qkv = exchange_sum(g_qkv)

    wide = hidden // 2
    early = [s_mid[:, :wide], after(s_down[:24], g_qkv), s_down[24:], s_mid[:, wide:]]
    early = lax.all_gather(jnp.concatenate(early, axis=1), ("zl", "y", "core"))
    g_in, g_down, g_out = emit(early.reshape((8, 2) + early.shape[1:]), width)
    mine = spread(s_qkv[:, :half].astype(BF16), ("zl", "y"))
    other = lax.ppermute(mine, "core", SWAP)
    low = lax.axis_index("core") == 0
    g_qkv = joined([jnp.where(low, mine, other), jnp.where(low, other, mine)])
    vec = s_qkv[:, half:]
    vec = (vec + lax.ppermute(vec, "core", SWAP)).reshape(-1)[:12 * piece].reshape(12, piece)

    ends = jnp.where(section == 0, d_h, out).reshape(shards, own_rows, width)
    home = jnp.zeros_like(ends)
    for d in range(shards):
        block = lax.dynamic_index_in_dim(ends, (shard + d) % shards, 0)
        block = turned(block, "fsdp", d) if d else block
        home = lax.dynamic_update_slice_in_dim(home, block, (shard + shards - d) % shards, 0)
    ends = home[:micro].astype(F32)
    return (
        ends[None, :, None],
        g_qkv.reshape(1, 192, -1),
        g_out[None],
        g_in[None],
        g_down[None],
        vec[None, :2],
        vec[None, 2:8],
        vec[None, 8:].reshape(1, -1),
    )


def solution(mesh):
    fine = Mesh(mesh.devices.reshape(2, 4, 2, 4, 2), ("section", "fsdp", "zl", "y", "core"))
    dp = ("zl", "y", "core")
    in_specs = (
        P("section", None, None, dp + ("fsdp",), None),
        P(None, None, dp),
        P("section", "fsdp", None),
        P("section", "fsdp", None),
        P("section", "fsdp", None),
        P("section", "fsdp", None),
        P("section", None, "fsdp"),
        P("section", None, "fsdp"),
        P("section", "fsdp"),
    )
    out_specs = (
        P("section", None, None, dp + ("fsdp",), None),
        P("section", "fsdp", None),
        P("section", "fsdp", None),
        P("section", "fsdp", None),
        P("section", "fsdp", None),
        P("section", None, "fsdp"),
        P("section", None, "fsdp"),
        P("section", "fsdp"),
    )
    return jax.shard_map(body, mesh=fine, in_specs=in_specs, out_specs=out_specs, check_vma=False)
```

```python
import functools

import jax
import jax.numpy as jnp
from jax import lax
from jax.experimental import pallas as pl
from jax.experimental.pallas import tpu as pltpu
from jax.sharding import Mesh, PartitionSpec as P

HD = 64
GROUP = 256
TILE = 768
CHUNK = 64
EPS = 1e-06
PEAK = 1.1e9
SWAP = [(0, 1), (1, 0)]
F32 = jnp.float32
BF16 = jnp.bfloat16
VMEM_BYTES = 48 * 1024 * 1024
VMEM_SMALL = 30 * 1024 * 1024


def dot_nn(a, b):
    return lax.dot_general(a, b, (((1,), (0,)), ((), ())), preferred_element_type=F32)


def dot_nt(a, b):
    return lax.dot_general(a, b, (((1,), (1,)), ((), ())), preferred_element_type=F32)


def dot_tn(a, b):
    return lax.dot_general(a, b, (((0,), (0,)), ((), ())), preferred_element_type=F32)


def chunks(rows, size=CHUNK):
    return [pl.ds(start, size) for start in range(0, rows, size)]


def attend_kernel(save, h_ref, wq_ref, wk_ref, wv_ref, par_ref, idc_ref, idr_ref, *rest):
    if save:
        ctx_ref, qkv_ref, lse_ref, mask_ref = rest
    else:
        ctx_ref, mask_ref = rest
    rows = h_ref.shape[0]

    @pl.when(pl.program_id(0) == 0)
    def _():
        for r in chunks(rows):
            mask_ref[r, :] = jnp.where(idc_ref[r, :] == idr_ref[...], 0.0, -1e30)

    h = h_ref[...]
    q = (dot_nn(h, wq_ref[...]) + par_ref[2:3, :]).astype(BF16)
    k = dot_nn(h, wk_ref[...]).astype(BF16)
    v = (dot_nn(h, wv_ref[...]) + par_ref[3:4, :]).astype(BF16)
    if save:
        qkv_ref[0] = q
        qkv_ref[1] = k
        qkv_ref[2] = v
    scaled = q * jnp.asarray(HD ** (-0.5), BF16)
    values_t = v.T
    parts = []
    for n in range(GROUP // HD):
        cols = slice(n * HD, (n + 1) * HD)
        st = dot_nt(k[:, cols], scaled[:, cols]) + mask_ref[...]
        top = jnp.max(st, axis=0, keepdims=True)
        e = jnp.exp(st - top)
        total = jnp.sum(e, axis=0, keepdims=True)
        parts.append(dot_nn(values_t[cols, :], e.astype(BF16)) * (1.0 / total))
        if save:
            lse_ref[n:n + 1, :] = top + jnp.log(total)
    ctx_ref[...] = jnp.concatenate(parts, axis=0).T.astype(BF16)


def attend(h, w_qkv, par, ids, save):
    rows, width = h.shape
    steps = width // GROUP
    out_shape = [jax.ShapeDtypeStruct((rows, width), BF16)]
    out_specs = [pl.BlockSpec((rows, GROUP), lambda j: (0, j))]
    if save:
        out_shape += [
            jax.ShapeDtypeStruct((3, rows, width), BF16),
            jax.ShapeDtypeStruct((8 * steps, rows), F32),
        ]
        out_specs += [
            pl.BlockSpec((3, rows, GROUP), lambda j: (0, 0, j)),
            pl.BlockSpec((8, rows), lambda j: (j, 0)),
        ]
    return pl.pallas_call(
        functools.partial(attend_kernel, save),
        grid=(steps,),
        in_specs=[
            pl.BlockSpec((rows, width), lambda j: (0, 0)),
            pl.BlockSpec((width, GROUP), lambda j: (0, j)),
            pl.BlockSpec((width, GROUP), lambda j: (0, j + steps)),
            pl.BlockSpec((width, GROUP), lambda j: (0, j + 2 * steps)),
            pl.BlockSpec((8, GROUP), lambda j: (0, j)),
            pl.BlockSpec((rows, 1), lambda j: (0, 0)),
            pl.BlockSpec((1, rows), lambda j: (0, 0)),
        ],
        out_specs=out_specs,
        out_shape=out_shape,
        scratch_shapes=[pltpu.VMEM((rows, rows), F32)],
        compiler_params=pltpu.CompilerParams(vmem_limit_bytes=VMEM_BYTES if save else VMEM_SMALL),
        cost_estimate=pl.CostEstimate(flops=int(10 * PEAK), bytes_accessed=0, transcendentals=0),
        name="attend_save" if save else "attend",
    )(h, w_qkv, w_qkv, w_qkv, par, ids[:, None], ids[None, :])


def normalise(u):
    center = u - jnp.mean(u, axis=-1, keepdims=True)
    inv = lax.rsqrt(jnp.mean(center * center, axis=-1, keepdims=True) + EPS)
    return center * inv, inv


def feed_kernel(save, h_ref, ctx_ref, wo_ref, wi_ref, wd_ref, par_ref, bi_ref, *rest):
    if save:
        (core_ref, out_ref, normed_ref, xh1_ref, inv1_ref, xh2_ref, inv2_ref, slope_ref, mine_ref, theirs_ref,
         acc_ref, inner_ref, act_ref) = rest
    else:
        out_ref, normed_ref, acc_ref, inner_ref, act_ref = rest
    rows = h_ref.shape[0]
    step = pl.program_id(0)

    @pl.when(step == 0)
    def _():
        acc_ref[...] = dot_nn(ctx_ref[...], wo_ref[...])
        for r in chunks(rows):
            first = h_ref[r, :].astype(F32) + (acc_ref[r, :] + par_ref[4:5, :])
            xh, inv = normalise(first)
            normed = (xh * par_ref[0:1, :] + par_ref[5:6, :]).astype(BF16)
            normed_ref[r, :] = normed
            acc_ref[r, :] = normed.astype(F32) + par_ref[6:7, :]
            if save:
                xh1_ref[r, :] = xh
                inv1_ref[r, :] = inv

    inner_ref[...] = dot_nn(normed_ref[...], wi_ref[...])
    for r in chunks(rows):
        t = inner_ref[r, :] + bi_ref[...]
        half = 0.5 * lax.erf(t * 0.7071067811865476) + 0.5
        act = (t * half).astype(BF16)
        act_ref[r, :] = act
        if save:
            bell = jnp.exp(-0.5 * (t * t)) * 0.3989422804014327
            slope_ref[r, :] = (half + t * bell).astype(BF16)
    acc_ref[...] += dot_nn(act_ref[...], wd_ref[...])
    if save:
        for core in range(2):
            @pl.when(core_ref[0] == core)
            def _():
                for n, ref in enumerate((mine_ref, theirs_ref) if core == 0 else (theirs_ref, mine_ref)):
                    ref[...] = act_ref[:, n * (TILE // 2):(n + 1) * (TILE // 2)]

    @pl.when(step == pl.num_programs(0) - 1)
    def _():
        for r in chunks(rows):
            xh, inv = normalise(acc_ref[r, :])
            out_ref[r, :] = (xh * par_ref[1:2, :] + par_ref[7:8, :]).astype(BF16)
            if save:
                xh2_ref[r, :] = xh
                inv2_ref[r, :] = inv


def feed(h, ctx, w_out, w_in, w_down, par, b_in, save, core=()):
    rows, width = h.shape
    hidden = w_in.shape[1]
    steps = hidden // TILE
    whole = lambda j: (0, 0)
    out_shape = [
        jax.ShapeDtypeStruct((rows, width), BF16),
        jax.ShapeDtypeStruct((rows, width), BF16),
    ]
    out_specs = [pl.BlockSpec((rows, width), whole), pl.BlockSpec((rows, width), whole)]
    scratch = [pltpu.VMEM((rows, width), F32), pltpu.VMEM((rows, TILE), F32)]
    if save:
        for shape in ((rows, width), (rows, 1), (rows, width), (rows, 1)):
            out_shape.append(jax.ShapeDtypeStruct(shape, F32))
            out_specs.append(pl.BlockSpec(shape, whole))
        out_shape.append(jax.ShapeDtypeStruct((rows, hidden), BF16))
        out_specs.append(pl.BlockSpec((rows, TILE), lambda j: (0, j)))
        out_shape += [jax.ShapeDtypeStruct((rows, hidden // 2), BF16)] * 2
        out_specs += [pl.BlockSpec((rows, TILE // 2), lambda j: (0, j))] * 2
    scratch.append(pltpu.VMEM((rows, TILE), BF16))
    return pl.pallas_call(
        functools.partial(feed_kernel, save),
        grid=(steps,),
        in_specs=[
            pl.BlockSpec((rows, width), whole),
            pl.BlockSpec((rows, width), whole),
            pl.BlockSpec((width, width), whole),
            pl.BlockSpec((width, TILE), lambda j: (0, j)),
            pl.BlockSpec((TILE, width), lambda j: (j, 0)),
            pl.BlockSpec((8, width), whole),
            pl.BlockSpec((1, TILE), lambda j: (0, j)),
        ] + [pl.BlockSpec(memory_space=pltpu.SMEM)] * len(core),
        out_specs=out_specs,
        out_shape=out_shape,
        scratch_shapes=scratch,
        compiler_params=pltpu.CompilerParams(vmem_limit_bytes=VMEM_BYTES if save else VMEM_SMALL),
        cost_estimate=pl.CostEstimate(flops=int((15 if save else 12) * PEAK), bytes_accessed=0, transcendentals=0),
        name="feed_save" if save else "feed",
    )(h, ctx, w_out, w_in, w_down, par, b_in, *core)


def norm_back(g, xh, inv, gain):
    weighted = g * gain
    mean = jnp.mean(weighted, axis=-1, keepdims=True)
    slope = jnp.mean(weighted * xh, axis=-1, keepdims=True)
    return (weighted - mean - xh * slope) * inv


def col_sum(rows):
    return jnp.sum(rows, axis=0, keepdims=True)


def norm_back_kernel(g_ref, xh_ref, inv_ref, par_ref, *rest):
    second_ref, branch_ref, sums_ref = rest[-3:]
    rows, width = g_ref.shape
    gain_sum = shift_sum = branch_sum = jnp.zeros((1, width), F32)
    for r in chunks(rows):
        g = g_ref[r, :].astype(F32)
        xh = xh_ref[r, :]
        second = norm_back(g, xh, inv_ref[r, :], par_ref[1:2, :])
        second_ref[r, :] = second
        branch = second.astype(BF16)
        branch_ref[r, :] = branch
        gain_sum += col_sum(g * xh)
        shift_sum += col_sum(g)
        branch_sum += col_sum(branch.astype(F32))
    sums_ref[...] = jnp.zeros_like(sums_ref)
    sums_ref[1:2, :] = gain_sum
    sums_ref[7:8, :] = shift_sum
    sums_ref[6:7, :] = branch_sum


def second_back(g, xh, inv, par, behind):
    rows, width = xh.shape
    vmem = pl.BlockSpec(memory_space=pltpu.VMEM)
    return pl.pallas_call(
        norm_back_kernel,
        in_specs=[vmem] * 4 + [pl.BlockSpec(memory_space=pl.ANY)] * len(behind),
        out_specs=[vmem] * 3,
        out_shape=[
            jax.ShapeDtypeStruct((rows, width), F32),
            jax.ShapeDtypeStruct((rows, width), BF16),
            jax.ShapeDtypeStruct((8, width), F32),
        ],
        compiler_params=pltpu.CompilerParams(vmem_limit_bytes=VMEM_BYTES),
        cost_estimate=pl.CostEstimate(flops=int(3 * PEAK), bytes_accessed=0, transcendentals=0),
        name="second_back",
    )(g, xh, inv, par, *behind)


def feed_back_kernel(save, g_ref, xh2_ref, inv2_ref, xh1_ref, inv1_ref, slope_ref, wd_ref, wi_ref, wo_ref,
                     par_ref, *rest):
    if save:
        first_ref, dctx_ref, inner_ref, att_ref, sums_ref, bsum_ref, acc_ref, dact_ref = rest[1:]
        branch_ref = xh2_ref
    else:
        first_ref, dctx_ref, acc_ref, dact_ref, branch_ref, inner_ref, att_ref = rest
    rows, width = g_ref.shape
    step = pl.program_id(0)

    @pl.when(step == 0)
    def _():
        if save:
            acc_ref[...] = g_ref[...]
            sums_ref[...] = jnp.zeros_like(sums_ref)
        else:
            for r in chunks(rows):
                g = g_ref[r, :].astype(F32)
                second = norm_back(g, xh2_ref[r, :], inv2_ref[r, :], par_ref[1:2, :])
                acc_ref[r, :] = second
                branch_ref[r, :] = second.astype(BF16)

    dact_ref[...] = dot_nt(branch_ref[...], wd_ref[...])
    bin_sum = jnp.zeros((1, dact_ref.shape[1]), F32)
    for r in chunks(rows):
        inner = (dact_ref[r, :] * slope_ref[r, :].astype(F32)).astype(BF16)
        if save:
            inner_ref[0, r, :] = inner
        else:
            inner_ref[r, :] = inner
        if save:
            bin_sum += col_sum(inner.astype(F32))
    if save:
        bsum_ref[...] = bin_sum
    acc_ref[...] += dot_nt(inner_ref[0] if save else inner_ref[...], wi_ref[...])

    @pl.when(step == pl.num_programs(0) - 1)
    def _():
        gain_sum = shift_sum = att_sum = jnp.zeros((1, width), F32)
        for r in chunks(rows):
            g = acc_ref[r, :]
            xh = xh1_ref[r, :]
            first = norm_back(g, xh, inv1_ref[r, :], par_ref[0:1, :])
            first_ref[r, :] = first
            att = first.astype(BF16)
            att_ref[r, :] = att
            if save:
                gain_sum += col_sum(g * xh)
                shift_sum += col_sum(g)
                att_sum += col_sum(att.astype(F32))
        if save:
            sums_ref[0:1, :] = gain_sum
            sums_ref[5:6, :] = shift_sum
            sums_ref[4:5, :] = att_sum
        dctx_ref[...] = dot_nt(att_ref[...], wo_ref[...]).astype(BF16)


def feed_back(g, kept, w_out, w_in, w_down, par, save, behind=()):
    xh1, inv1, xh2, inv2, slope = kept
    rows, width = xh1.shape
    hidden = slope.shape[1]
    steps = hidden // TILE
    whole = lambda j: (0, 0)
    full = pl.BlockSpec((rows, width), whole)
    tile = pl.BlockSpec((rows, TILE), lambda j: (0, j))
    out_shape = [jax.ShapeDtypeStruct((rows, width), F32), jax.ShapeDtypeStruct((rows, width), BF16)]
    out_specs = [full, full]
    scratch = [pltpu.VMEM((rows, width), F32), pltpu.VMEM((rows, TILE), F32)]
    if save:
        out_shape += [
            jax.ShapeDtypeStruct((2, rows, hidden // 2), BF16),
            jax.ShapeDtypeStruct((rows, width), BF16),
            jax.ShapeDtypeStruct((8, width), F32),
            jax.ShapeDtypeStruct((1, hidden), F32),
        ]
        out_specs += [
            pl.BlockSpec((1, rows, TILE), lambda j: (j // (steps // 2), 0, j % (steps // 2))), full,
            pl.BlockSpec((8, width), whole),
            pl.BlockSpec((1, TILE), lambda j: (0, j)),
        ]
    else:
        scratch += [pltpu.VMEM((rows, width), BF16), pltpu.VMEM((rows, TILE), BF16), pltpu.VMEM((rows, width), BF16)]
    return pl.pallas_call(
        functools.partial(feed_back_kernel, save),
        grid=(steps,),
        in_specs=[
            full, full, pl.BlockSpec((rows, 1), whole), full, pl.BlockSpec((rows, 1), whole), tile,
            pl.BlockSpec((TILE, width), lambda j: (j, 0)),
            pl.BlockSpec((width, TILE), lambda j: (0, j)),
            pl.BlockSpec((width, width), whole),
            pl.BlockSpec((8, width), whole),
        ] + [pl.BlockSpec(memory_space=pl.ANY)] * len(behind),
        out_specs=out_specs,
        out_shape=out_shape,
        scratch_shapes=scratch,
        compiler_params=pltpu.CompilerParams(vmem_limit_bytes=VMEM_BYTES),
        cost_estimate=pl.CostEstimate(flops=int((15 if save else 12) * PEAK), bytes_accessed=0, transcendentals=0),
        name="feed_back_save" if save else "feed_back",
    )(g, xh2, inv2, xh1, inv1, slope, w_down, w_in, w_out, par, *behind)


def attend_back_kernel(save, qkv_ref, dctx_ref, lse_ref, idc_ref, idr_ref, wq_ref, wk_ref, wv_ref, first_ref, *rest):
    if save:
        dh_ref, dqkv_ref, sums_ref, mask_ref, acc_ref = rest[-5:]
    else:
        dh_ref, mask_ref, acc_ref = rest
    rows = first_ref.shape[0]
    step = pl.program_id(0)

    @pl.when(step == 0)
    def _():
        for r in chunks(rows):
            mask_ref[r, :] = jnp.where(idc_ref[r, :] == idr_ref[...], 0.0, -1e30)
        acc_ref[...] = first_ref[...]

    scale = HD ** (-0.5)
    q = qkv_ref[0] * jnp.asarray(scale, BF16)
    k = qkv_ref[1]
    v = qkv_ref[2]
    dctx = dctx_ref[...]
    keys_t = k.T
    dq_t = []
    dk = []
    dv = []
    for n in range(GROUP // HD):
        cols = slice(n * HD, (n + 1) * HD)
        lse = lse_ref[n:n + 1, :]
        st = dot_nt(k[:, cols], q[:, cols]) + mask_ref[...]
        pt = jnp.exp(st - lse)
        dpt = dot_nt(v[:, cols], dctx[:, cols])
        row = jnp.sum(pt * dpt, axis=0, keepdims=True)
        dst = (pt * (dpt - row)).astype(BF16)
        dv.append(dot_nn(pt.astype(BF16), dctx[:, cols]))
        dk.append(dot_nn(dst, q[:, cols]))
        dq_t.append(dot_nn(keys_t[cols, :], dst))
    dq = (jnp.concatenate(dq_t, axis=0).T * scale).astype(BF16)
    dk = jnp.concatenate(dk, axis=1).astype(BF16)
    dv = jnp.concatenate(dv, axis=1).astype(BF16)
    if save:
        for n, part in enumerate((dq, dk, dv)):
            offset = n * first_ref.shape[1] + step * GROUP
            dqkv_ref[:, pl.ds(pl.multiple_of(offset, GROUP), GROUP)] = part
        sums_ref[...] = jnp.zeros_like(sums_ref)
        sums_ref[2:3, :] = col_sum(dq.astype(F32))
        sums_ref[3:4, :] = col_sum(dv.astype(F32))
    acc_ref[...] += dot_nt(dq, wq_ref[...]) + dot_nt(dk, wk_ref[...]) + dot_nt(dv, wv_ref[...])

    @pl.when(step == pl.num_programs(0) - 1)
    def _():
        dh_ref[...] = acc_ref[...].astype(BF16)


def attend_back(qkv, dctx, lse, ids, w_qkv, first, save, behind=()):
    rows, width = first.shape
    steps = width // GROUP
    whole = lambda j: (0, 0)
    full = pl.BlockSpec((rows, width), whole)
    out_shape = [jax.ShapeDtypeStruct((rows, width), BF16)]
    out_specs = [full]
    if save:
        out_shape += [jax.ShapeDtypeStruct((rows, 3 * width), BF16), jax.ShapeDtypeStruct((8, width), F32)]
        out_specs += [
            pl.BlockSpec((rows, 3 * width), whole),
            pl.BlockSpec((8, GROUP), lambda j: (0, j)),
        ]
    return pl.pallas_call(
        functools.partial(attend_back_kernel, save),
        grid=(steps,),
        in_specs=[
            pl.BlockSpec((3, rows, GROUP), lambda j: (0, 0, j)),
            pl.BlockSpec((rows, GROUP), lambda j: (0, j)),
            pl.BlockSpec((8, rows), lambda j: (j, 0)),
            pl.BlockSpec((rows, 1), whole),
            pl.BlockSpec((1, rows), whole),
            pl.BlockSpec((width, GROUP), lambda j: (0, j)),
            pl.BlockSpec((width, GROUP), lambda j: (0, j + steps)),
            pl.BlockSpec((width, GROUP), lambda j: (0, j + 2 * steps)),
            full,
        ] + [pl.BlockSpec(memory_space=pl.ANY)] * len(behind),
        out_specs=out_specs,
        out_shape=out_shape,
        scratch_shapes=[pltpu.VMEM((rows, rows), F32), pltpu.VMEM((rows, width), F32)],
        compiler_params=pltpu.CompilerParams(vmem_limit_bytes=VMEM_BYTES),
        cost_estimate=pl.CostEstimate(flops=int(14 * PEAK), bytes_accessed=0, transcendentals=0),
        name="attend_back_save" if save else "attend_back",
    )(qkv, dctx, lse, ids[:, None], ids[None, :], w_qkv, w_qkv, w_qkv, first, *behind)


def lefts_kernel(core_ref, *refs):
    sources, outs = refs[:8], refs[9:]
    rows = sources[0].shape[0]
    for n, out in enumerate(outs):
        own, other = sources[2 * n], sources[2 * n + 1]
        out[:, :rows] = own[...].T
        out[:, rows:] = other[...].T


def lefts(core, pairs, act, act_other, behind):
    rows, width = pairs[0].shape
    steps = width // GROUP
    wide = act.shape[1] // steps
    tile = pl.BlockSpec((rows, GROUP), lambda i, c: (0, i))
    return pl.pallas_call(
        lefts_kernel,
        grid_spec=pltpu.PrefetchScalarGridSpec(
            num_scalar_prefetch=1,
            grid=(steps,),
            in_specs=[tile] * len(pairs) + [
                pl.BlockSpec((rows, wide), lambda i, c: (0, i)),
                pl.BlockSpec((rows, wide), lambda i, c: (0, i)),
                pl.BlockSpec(memory_space=pl.ANY),
            ],
            out_specs=[pl.BlockSpec((GROUP, 2 * rows), lambda i, c: (i, 0))] * (len(pairs) // 2)
            + [pl.BlockSpec((wide, 2 * rows), lambda i, c: (i, 0))],
        ),
        out_shape=[jax.ShapeDtypeStruct((width, 2 * rows), BF16)] * (len(pairs) // 2)
        + [jax.ShapeDtypeStruct((act.shape[1], 2 * rows), BF16)],
        compiler_params=pltpu.CompilerParams(vmem_limit_bytes=VMEM_BYTES),
        cost_estimate=pl.CostEstimate(flops=int(10 * PEAK), bytes_accessed=0, transcendentals=0),
        name="lefts",
    )(core, *pairs, act, act_other, behind)


def grad_kernel(count, core_ref, *refs):
    extra_ref, out_ref = refs[3 * count:-1], refs[-1]
    at = 0
    for n in range(count):
        left, own, other = refs[3 * n:3 * n + 3]
        rows, cols = other.shape
        mine = own[0] if len(own.shape) == 3 else own[...]
        total = dot_nn(left[:, :rows], mine) + dot_nn(left[:, rows:], other[...])
        out_ref[:, at:at + cols] = total.astype(BF16)
        at += cols
    if extra_ref:
        out_ref[:, at:] = extra_ref[0][...]


def grad(core, parts, extra, name):
    size = min(512, GROUP * (parts[0][0].shape[0] // 768))
    height = parts[0][0].shape[0]
    in_specs, args, cols = [], [], 0
    for left, own, other in parts:
        rows, part = other.shape
        in_specs.append(pl.BlockSpec((size, left.shape[1]), lambda i, c: (i, 0)))
        if own.ndim == 3:
            in_specs.append(pl.BlockSpec((1, rows, part), lambda i, c: (c[0], 0, 0)))
        elif own.shape[1] == part:
            in_specs.append(pl.BlockSpec((rows, part), lambda i, c: (0, 0)))
        else:
            in_specs.append(pl.BlockSpec((rows, part), lambda i, c: (0, c[0])))
        in_specs.append(pl.BlockSpec((rows, part), lambda i, c: (0, 0)))
        args += [left, own, other]
        cols += part
    if extra is not None:
        in_specs.append(pl.BlockSpec((size, extra.shape[1]), lambda i, c: (i, 0)))
        args.append(extra)
        cols += extra.shape[1]
    return pl.pallas_call(
        functools.partial(grad_kernel, len(parts)),
        grid_spec=pltpu.PrefetchScalarGridSpec(
            num_scalar_prefetch=1,
            grid=(height // size,),
            in_specs=in_specs,
            out_specs=pl.BlockSpec((size, cols), lambda i, c: (i, 0)),
        ),
        out_shape=jax.ShapeDtypeStruct((height, cols), BF16),
        compiler_params=pltpu.CompilerParams(vmem_limit_bytes=VMEM_BYTES),
        cost_estimate=pl.CostEstimate(flops=int(1 * PEAK), bytes_accessed=0, transcendentals=0),
        name=name,
    )(core, *args)


def turned(block, axis, by):
    count = lax.axis_size(axis)
    return lax.ppermute(block, axis, [(i, (i + by) % count) for i in range(count)])


def around(block, axis):
    return [block] + [turned(block, axis, d) for d in range(1, lax.axis_size(axis))]


def place_kernel(plan, outs, at_ref, *refs):
    sources, out_refs, sems = refs[:len(plan)], refs[-1 - outs:-1], refs[-1]
    copies = []
    for n, (ref, (which, pick, where)) in enumerate(zip(sources, plan)):
        copies.append(pltpu.make_async_copy(pick(ref), where(out_refs[which], at_ref), sems.at[n]))
    for copy in copies:
        copy.start()
    for copy in copies:
        copy.wait()


def place(at, groups, name, behind=()):
    plan = [(n, pick, where) for n, (_, pieces) in enumerate(groups) for _, pick, where in pieces]
    arrays = [piece[0] for _, pieces in groups for piece in pieces]
    anywhere = pl.BlockSpec(memory_space=pl.ANY)
    return pl.pallas_call(
        functools.partial(place_kernel, plan, len(groups)),
        in_specs=[pl.BlockSpec(memory_space=pltpu.SMEM)] + [anywhere] * (len(arrays) + len(behind)),
        out_specs=[pl.BlockSpec(memory_space=pltpu.VMEM)] * len(groups),
        out_shape=[jax.ShapeDtypeStruct(shape, BF16) for shape, _ in groups],
        scratch_shapes=[pltpu.SemaphoreType.DMA((len(arrays),))],
        compiler_params=pltpu.CompilerParams(vmem_limit_bytes=VMEM_SMALL),
        cost_estimate=pl.CostEstimate(flops=int(5 * PEAK), bytes_accessed=0, transcendentals=0),
        name=name,
    )(at, *arrays, *behind)


X, Y, Z, C = range(4)


def after(block, other):
    return block + (other[(slice(0, 1),) * other.ndim].reshape(()) * 0).astype(block.dtype)


def spread(block, axis):
    count = lax.axis_size(axis)
    return lax.all_to_all(jnp.broadcast_to(block[None], (count,) + block.shape), axis, 0, 0, tiled=True)


def pieces_x(block):
    return [
        (
            part,
            lambda ref, d=d: ref.at[d],
            lambda out, at, d=d, e=e: out.at[(at[X] + 4 - d) % 4, (at[C] + e) % 2],
        )
        for e, part in enumerate(around(block, "core"))
        for d in range(4)
    ]


def pieces_around(blocks):
    return [
        (
            part,
            lambda ref: ref,
            lambda out, at, d=d, e=e: out.at[(at[X] + 4 - d) % 4, (at[C] + e) % 2],
        )
        for d, block in enumerate(blocks)
        for e, part in enumerate(around(block, "core"))
    ]


def pieces_xy(block):
    part = block.shape[2]
    return [
        (
            swapped,
            lambda ref, d=d: ref.at[d],
            lambda out, at, d=d, e=e, g=g: out.at[
                (at[X] + 4 - d) % 4, (at[C] + e) % 2, :,
                pl.ds(pl.multiple_of((at[Y] + 4 - g) % 4 * part, 128), part),
            ],
        )
        for g, moved in enumerate(around(block, "y"))
        for e, swapped in enumerate(around(moved, "core"))
        for d in range(4)
    ]


def pieces_xz(block):
    return [
        (
            swapped,
            lambda ref, d=d: ref.at[d],
            lambda out, at, d=d, e=e, g=g: out.at[
                (at[X] + 4 - d) % 4, (at[C] + e) % 2, (at[Z] + g) % 2
            ],
        )
        for g, moved in enumerate(around(block, "zl"))
        for e, swapped in enumerate(around(moved, "core"))
        for d in range(4)
    ]


def other_core(block):
    return lax.ppermute(block, "core", SWAP)


def other_half(block, behind=None):
    there = 1 - lax.axis_index("core")
    if block.ndim == 3:
        send = lax.dynamic_index_in_dim(block, there, 0, keepdims=False)
    else:
        half = block.shape[1] // 2
        send = lax.dynamic_slice_in_dim(block, there * half, half, 1)
    return other_core(send if behind is None else after(send, behind))


WIDE = ("fsdp", "zl", "y")


def exchange_sum(block):
    return jnp.sum(lax.all_to_all(block, WIDE, 0, 0, tiled=True).astype(F32), axis=0)


def emit_kernel(in_ref, down_ref, out_ref, g_in_ref, g_down_ref, g_out_ref):
    rows = g_in_ref.shape[0]
    g_in_ref[...] = in_ref[...].astype(F32).reshape(rows, -1)
    g_out_ref[...] = out_ref[...].astype(F32).reshape(rows, -1)
    pieces, _, rows, cols = down_ref.shape
    block = down_ref[...].astype(F32)
    for n in range(2 * pieces):
        at = (n % 2) * (cols // 2)
        g_down_ref[n * rows:(n + 1) * rows, :] = block[n // 2, 0, :, at:at + cols // 2]


def emit(early, width):
    pieces, cores, rows, _ = early.shape
    half, steps = width // 2, 2
    step = pieces // steps
    return pl.pallas_call(
        emit_kernel,
        grid=(steps, cores),
        in_specs=[
            pl.BlockSpec((step, 1, rows, 4 * half), lambda i, c: (i, c, 0, 0)),
            pl.BlockSpec((step, 1, rows, 4 * half), lambda i, c: (i, c, 0, 1)),
            pl.BlockSpec((step, 1, rows, half), lambda i, c: (i, c, 0, 8)),
        ],
        out_specs=[
            pl.BlockSpec((step * rows, 4 * half), lambda i, c: (i, c)),
            pl.BlockSpec((2 * step * rows, 2 * half), lambda i, c: (c * steps + i, 0)),
            pl.BlockSpec((step * rows, half), lambda i, c: (i, c)),
        ],
        out_shape=[
            jax.ShapeDtypeStruct((pieces * rows, 8 * half), F32),
            jax.ShapeDtypeStruct((2 * cores * pieces * rows, 2 * half), F32),
            jax.ShapeDtypeStruct((pieces * rows, 2 * half), F32),
        ],
        cost_estimate=pl.CostEstimate(flops=int(5 * PEAK), bytes_accessed=0, transcendentals=0),
        name="emit",
    )(early, early, early)


def joined(halves):
    return jnp.concatenate(halves, axis=-1).astype(F32)


def body(boundary, seq_ids, w_qkv, w_out, w_in, w_down, gains, biases, b_in):
    section = lax.axis_index("section")
    shard = lax.axis_index("fsdp")
    own = boundary[0, :, 0]
    micro, own_rows, width = own.shape
    shards = lax.axis_size("fsdp")
    rows = own_rows * shards
    hidden = b_in.shape[1] * shards
    piece = width // shards
    at = jnp.stack([lax.axis_index(name) for name in ("fsdp", "y", "zl", "core")]).astype(jnp.int32)

    small = jnp.concatenate([gains[0], biases[0], b_in[0].reshape(-1, piece)])
    small = jnp.pad(small.reshape(-1, width), ((0, 13), (0, 0)))
    padded = jnp.concatenate([own, jnp.zeros((shards - micro,) + own.shape[1:], BF16)])
    padded = jnp.concatenate([padded, jnp.broadcast_to(small[None], (shards,) + small.shape)], axis=1)

    half, part, cols = piece // 2, w_down.shape[1] // 4, w_in.shape[2] // 4
    own_in = lax.dynamic_slice(w_in[0], (at[C] * half, at[Y] * cols), (half, cols))
    own_down = lax.dynamic_slice_in_dim(w_down[0], (at[C] * 2 + at[Z]) * part, part, 0)
    own_out = lax.dynamic_slice_in_dim(w_out[0], at[C] * half, half, 0)
    own_qkv = lax.dynamic_slice_in_dim(w_qkv[0], at[C] * half, half, 0)
    in_blocks = around(jnp.concatenate([own_in, own_out]), "fsdp")
    down_blocks = around(after(own_down, in_blocks[1]), "fsdp")
    qkv_blocks = around(after(own_qkv, down_blocks[1]), "fsdp")
    padded = lax.all_to_all(padded, "fsdp", 0, 0, tiled=True)
    in_block = jnp.stack([block[:half] for block in in_blocks])
    out_block = jnp.stack([block[half:] for block in in_blocks])
    shape_x = (4, 2, half)
    (full_qkv,) = place(at, [(shape_x + (3 * width,), pieces_around(qkv_blocks))], "place_qkv")
    full_qkv = full_qkv.reshape(width, 3 * width)

    slot = padded[:, :own_rows].reshape(rows, width)
    small = padded[:, own_rows:own_rows + 3].reshape(shards, 12, piece)
    par = jnp.swapaxes(small[:, :8], 0, 1).reshape(8, width).astype(F32)
    bias_in = small[:, 8:].reshape(1, hidden).astype(F32)
    ids = lax.dynamic_index_in_dim(seq_ids[:, 0], jnp.minimum(shard, micro - 1), 0, keepdims=False)

    (ctx,) = attend(slot, full_qkv, par, ids, False)
    full_in, full_down, full_out = place(
        at,
        [
            (shape_x + (hidden,), pieces_xy(in_block)),
            ((4, 2, 2, part, width), pieces_xz(jnp.stack(down_blocks))),
            (shape_x + (width,), pieces_x(out_block)),
        ],
        "place_rest",
        [ctx],
    )
    full_in = full_in.reshape(width, hidden)
    full_down = full_down.reshape(hidden, width)
    full_out = full_out.reshape(width, width)
    middle = feed(slot, ctx, full_out, full_in, full_down, par, bias_in, False)[0]
    arrived = lax.ppermute(middle, "section", [(0, 1)])

    h = jnp.where(section == 0, slot, arrived)
    ctx, qkv, lse = attend(h, full_qkv, par, ids, True)
    core = at[C:]
    out, normed, xh1, inv1, xh2, inv2, slope, act, act_theirs = feed(
        h, ctx, full_out, full_in, full_down, par, bias_in, True, [core]
    )
    kept = (xh1, inv1, xh2, inv2, slope)

    cot = jnp.where(ids[:, None] >= 0, slot, jnp.zeros_like(slot))
    first, dctx = feed_back(cot, kept, full_out, full_in, full_down, par, False)
    (d_middle,) = attend_back(qkv, dctx, lse, ids, full_qkv, first, False)
    returned = lax.ppermute(d_middle, "section", [(1, 0)])

    pairs = [part for block in (h, normed, ctx) for part in (block, other_core(block))]
    h2, normed2, ctx2, act2 = lefts(core, pairs, act, other_core(act_theirs), d_middle)

    g = jnp.where(section == 0, returned, after(cot, h2))
    second, branch, sums2 = second_back(g, xh2, inv2, par, [h2, normed2, ctx2, act2])
    g_down = grad(core, [(act2, branch, other_core(branch))], None, "grad_down")
    s_down = exchange_sum(g_down.reshape(32, 48, width)).astype(BF16)
    first, dctx, inner, att, sums1, bin_sums = feed_back(
        second, (xh1, inv1, branch, inv2, slope), full_out, full_in, full_down, par, True, [g_down]
    )
    g_mid = grad(
        core, [(normed2, inner, other_half(inner)), (ctx2, att, other_half(att))], None, "grad_mid"
    )
    s_mid = exchange_sum(g_mid.reshape(32, 24, -1)).astype(BF16)
    d_h, dqkv, sums0 = attend_back(qkv, dctx, lse, ids, full_qkv, first, True, [g_mid, s_down])

    vec = (sums0 + sums1 + sums2).reshape(8, shards, piece)
    vec = jnp.concatenate([jnp.swapaxes(vec, 0, 1), bin_sums.reshape(shards, -1, piece)], axis=1)
    vec = jnp.pad(vec.reshape(shards, -1).astype(BF16), ((0, 0), (0, 768))).reshape(shards, 1, 24, 128)
    vec = jnp.broadcast_to(vec, (shards, 8, 24, 128)).reshape(768, 128)
    g_qkv = grad(core, [(h2, dqkv, other_half(dqkv))], vec, "grad_qkv").reshape(32, 24, -1)
    half = g_qkv.shape[2] - 128
    s_qkv = exchange_sum(g_qkv)

    wide = hidden // 2
    early = [s_mid[:, :wide], after(s_down[:24], g_qkv), s_down[24:], s_mid[:, wide:]]
    early = lax.all_gather(jnp.concatenate(early, axis=1), ("zl", "y", "core"))
    g_in, g_down, g_out = emit(early.reshape((8, 2) + early.shape[1:]), width)
    mine = spread(s_qkv[:, :half].astype(BF16), ("zl", "y"))
    other = lax.ppermute(mine, "core", SWAP)
    low = lax.axis_index("core") == 0
    g_qkv = joined([jnp.where(low, mine, other), jnp.where(low, other, mine)])
    vec = s_qkv[:, half:]
    vec = (vec + lax.ppermute(vec, "core", SWAP)).reshape(-1)[:12 * piece].reshape(12, piece)

    ends = jnp.where(section == 0, d_h, out).reshape(shards, own_rows, width)
    home = jnp.zeros_like(ends)
    for d in range(shards):
        block = lax.dynamic_index_in_dim(ends, (shard + d) % shards, 0)
        block = turned(block, "fsdp", d) if d else block
        home = lax.dynamic_update_slice_in_dim(home, block, (shard + shards - d) % shards, 0)
    ends = home[:micro].astype(F32)
    return (
        ends[None, :, None],
        g_qkv.reshape(1, 192, -1),
        g_out[None],
        g_in[None],
        g_down[None],
        vec[None, :2],
        vec[None, 2:8],
        vec[None, 8:].reshape(1, -1),
    )


def solution(mesh):
    fine = Mesh(mesh.devices.reshape(2, 4, 2, 4, 2), ("section", "fsdp", "zl", "y", "core"))
    dp = ("zl", "y", "core")
    in_specs = (
        P("section", None, None, dp + ("fsdp",), None),
        P(None, None, dp),
        P("section", "fsdp", None),
        P("section", "fsdp", None),
        P("section", "fsdp", None),
        P("section", "fsdp", None),
        P("section", None, "fsdp"),
        P("section", None, "fsdp"),
        P("section", "fsdp"),
    )
    out_specs = (
        P("section", None, None, dp + ("fsdp",), None),
        P("section", "fsdp", None),
        P("section", "fsdp", None),
        P("section", "fsdp", None),
        P("section", "fsdp", None),
        P("section", None, "fsdp"),
        P("section", None, "fsdp"),
        P("section", "fsdp"),
    )
    return jax.shard_map(body, mesh=fine, in_specs=in_specs, out_specs=out_specs, check_vma=False)
```

```python
import functools

import jax
import jax.numpy as jnp
from jax import lax
from jax.experimental import pallas as pl
from jax.experimental.pallas import tpu as pltpu
from jax.sharding import Mesh, PartitionSpec as P

HD = 64
GROUP = 256
TILE = 768
CHUNK = 64
EPS = 1e-06
PEAK = 1.1e9
SWAP = [(0, 1), (1, 0)]
F32 = jnp.float32
BF16 = jnp.bfloat16
VMEM_BYTES = 48 * 1024 * 1024
VMEM_SMALL = 30 * 1024 * 1024


def dot_nn(a, b):
    return lax.dot_general(a, b, (((1,), (0,)), ((), ())), preferred_element_type=F32)


def dot_nt(a, b):
    return lax.dot_general(a, b, (((1,), (1,)), ((), ())), preferred_element_type=F32)


def dot_tn(a, b):
    return lax.dot_general(a, b, (((0,), (0,)), ((), ())), preferred_element_type=F32)


def chunks(rows, size=CHUNK):
    return [pl.ds(start, size) for start in range(0, rows, size)]


def attend_kernel(save, h_ref, wq_ref, wk_ref, wv_ref, par_ref, idc_ref, idr_ref, *rest):
    if save:
        ctx_ref, qkv_ref, lse_ref, mask_ref = rest
    else:
        ctx_ref, mask_ref = rest
    rows = h_ref.shape[0]

    @pl.when(pl.program_id(0) == 0)
    def _():
        for r in chunks(rows):
            mask_ref[r, :] = jnp.where(idc_ref[r, :] == idr_ref[...], 0.0, -1e30)

    h = h_ref[...]
    q = (dot_nn(h, wq_ref[...]) + par_ref[2:3, :]).astype(BF16)
    k = dot_nn(h, wk_ref[...]).astype(BF16)
    v = (dot_nn(h, wv_ref[...]) + par_ref[3:4, :]).astype(BF16)
    if save:
        qkv_ref[0] = q
        qkv_ref[1] = k
        qkv_ref[2] = v
    scaled = q * jnp.asarray(HD ** (-0.5), BF16)
    values_t = v.T
    parts = []
    for n in range(GROUP // HD):
        cols = slice(n * HD, (n + 1) * HD)
        st = dot_nt(k[:, cols], scaled[:, cols]) + mask_ref[...]
        top = jnp.max(st, axis=0, keepdims=True)
        e = jnp.exp(st - top)
        total = jnp.sum(e, axis=0, keepdims=True)
        parts.append(dot_nn(values_t[cols, :], e.astype(BF16)) * (1.0 / total))
        if save:
            lse_ref[n:n + 1, :] = top + jnp.log(total)
    ctx_ref[...] = jnp.concatenate(parts, axis=0).T.astype(BF16)


def attend(h, w_qkv, par, ids, save):
    rows, width = h.shape
    steps = width // GROUP
    out_shape = [jax.ShapeDtypeStruct((rows, width), BF16)]
    out_specs = [pl.BlockSpec((rows, GROUP), lambda j: (0, j))]
    if save:
        out_shape += [
            jax.ShapeDtypeStruct((3, rows, width), BF16),
            jax.ShapeDtypeStruct((8 * steps, rows), F32),
        ]
        out_specs += [
            pl.BlockSpec((3, rows, GROUP), lambda j: (0, 0, j)),
            pl.BlockSpec((8, rows), lambda j: (j, 0)),
        ]
    return pl.pallas_call(
        functools.partial(attend_kernel, save),
        grid=(steps,),
        in_specs=[
            pl.BlockSpec((rows, width), lambda j: (0, 0)),
            pl.BlockSpec((width, GROUP), lambda j: (0, j)),
            pl.BlockSpec((width, GROUP), lambda j: (0, j + steps)),
            pl.BlockSpec((width, GROUP), lambda j: (0, j + 2 * steps)),
            pl.BlockSpec((8, GROUP), lambda j: (0, j)),
            pl.BlockSpec((rows, 1), lambda j: (0, 0)),
            pl.BlockSpec((1, rows), lambda j: (0, 0)),
        ],
        out_specs=out_specs,
        out_shape=out_shape,
        scratch_shapes=[pltpu.VMEM((rows, rows), F32)],
        compiler_params=pltpu.CompilerParams(vmem_limit_bytes=VMEM_BYTES if save else VMEM_SMALL),
        cost_estimate=pl.CostEstimate(flops=int(10 * PEAK), bytes_accessed=0, transcendentals=0),
        name="attend_save" if save else "attend",
    )(h, w_qkv, w_qkv, w_qkv, par, ids[:, None], ids[None, :])


def normalise(u):
    center = u - jnp.mean(u, axis=-1, keepdims=True)
    inv = lax.rsqrt(jnp.mean(center * center, axis=-1, keepdims=True) + EPS)
    return center * inv, inv


def feed_kernel(save, h_ref, ctx_ref, wo_ref, wi_ref, wd_ref, par_ref, bi_ref, *rest):
    if save:
        (core_ref, out_ref, normed_ref, xh1_ref, inv1_ref, xh2_ref, inv2_ref, slope_ref, mine_ref, theirs_ref,
         acc_ref, inner_ref, act_ref) = rest
    else:
        out_ref, normed_ref, acc_ref, inner_ref, act_ref = rest
    rows = h_ref.shape[0]
    step = pl.program_id(0)

    @pl.when(step == 0)
    def _():
        acc_ref[...] = dot_nn(ctx_ref[...], wo_ref[...])
        for r in chunks(rows):
            first = h_ref[r, :].astype(F32) + (acc_ref[r, :] + par_ref[4:5, :])
            xh, inv = normalise(first)
            normed = (xh * par_ref[0:1, :] + par_ref[5:6, :]).astype(BF16)
            normed_ref[r, :] = normed
            acc_ref[r, :] = normed.astype(F32) + par_ref[6:7, :]
            if save:
                xh1_ref[r, :] = xh
                inv1_ref[r, :] = inv

    inner_ref[...] = dot_nn(normed_ref[...], wi_ref[...])
    for r in chunks(rows):
        t = inner_ref[r, :] + bi_ref[...]
        half = 0.5 * lax.erf(t * 0.7071067811865476) + 0.5
        act = (t * half).astype(BF16)
        act_ref[r, :] = act
        if save:
            bell = jnp.exp(-0.5 * (t * t)) * 0.3989422804014327
            slope_ref[r, :] = (half + t * bell).astype(BF16)
    acc_ref[...] += dot_nn(act_ref[...], wd_ref[...])
    if save:
        for core in range(2):
            @pl.when(core_ref[0] == core)
            def _():
                for n, ref in enumerate((mine_ref, theirs_ref) if core == 0 else (theirs_ref, mine_ref)):
                    ref[...] = act_ref[:, n * (TILE // 2):(n + 1) * (TILE // 2)]

    @pl.when(step == pl.num_programs(0) - 1)
    def _():
        for r in chunks(rows):
            xh, inv = normalise(acc_ref[r, :])
            out_ref[r, :] = (xh * par_ref[1:2, :] + par_ref[7:8, :]).astype(BF16)
            if save:
                xh2_ref[r, :] = xh
                inv2_ref[r, :] = inv


def feed(h, ctx, w_out, w_in, w_down, par, b_in, save, core=()):
    rows, width = h.shape
    hidden = w_in.shape[1]
    steps = hidden // TILE
    whole = lambda j: (0, 0)
    out_shape = [
        jax.ShapeDtypeStruct((rows, width), BF16),
        jax.ShapeDtypeStruct((rows, width), BF16),
    ]
    out_specs = [pl.BlockSpec((rows, width), whole), pl.BlockSpec((rows, width), whole)]
    scratch = [pltpu.VMEM((rows, width), F32), pltpu.VMEM((rows, TILE), F32)]
    if save:
        for shape in ((rows, width), (rows, 1), (rows, width), (rows, 1)):
            out_shape.append(jax.ShapeDtypeStruct(shape, F32))
            out_specs.append(pl.BlockSpec(shape, whole))
        out_shape.append(jax.ShapeDtypeStruct((rows, hidden), BF16))
        out_specs.append(pl.BlockSpec((rows, TILE), lambda j: (0, j)))
        out_shape += [jax.ShapeDtypeStruct((rows, hidden // 2), BF16)] * 2
        out_specs += [pl.BlockSpec((rows, TILE // 2), lambda j: (0, j))] * 2
    scratch.append(pltpu.VMEM((rows, TILE), BF16))
    return pl.pallas_call(
        functools.partial(feed_kernel, save),
        grid=(steps,),
        in_specs=[
            pl.BlockSpec((rows, width), whole),
            pl.BlockSpec((rows, width), whole),
            pl.BlockSpec((width, width), whole),
            pl.BlockSpec((width, TILE), lambda j: (0, j)),
            pl.BlockSpec((TILE, width), lambda j: (j, 0)),
            pl.BlockSpec((8, width), whole),
            pl.BlockSpec((1, TILE), lambda j: (0, j)),
        ] + [pl.BlockSpec(memory_space=pltpu.SMEM)] * len(core),
        out_specs=out_specs,
        out_shape=out_shape,
        scratch_shapes=scratch,
        compiler_params=pltpu.CompilerParams(vmem_limit_bytes=VMEM_BYTES if save else VMEM_SMALL),
        cost_estimate=pl.CostEstimate(flops=int((15 if save else 12) * PEAK), bytes_accessed=0, transcendentals=0),
        name="feed_save" if save else "feed",
    )(h, ctx, w_out, w_in, w_down, par, b_in, *core)


def norm_back(g, xh, inv, gain):
    weighted = g * gain
    mean = jnp.mean(weighted, axis=-1, keepdims=True)
    slope = jnp.mean(weighted * xh, axis=-1, keepdims=True)
    return (weighted - mean - xh * slope) * inv


def col_sum(rows):
    return jnp.sum(rows, axis=0, keepdims=True)


def norm_back_kernel(g_ref, xh_ref, inv_ref, par_ref, *rest):
    second_ref, branch_ref, sums_ref = rest[-3:]
    rows, width = g_ref.shape
    gain_sum = shift_sum = branch_sum = jnp.zeros((1, width), F32)
    for r in chunks(rows):
        g = g_ref[r, :].astype(F32)
        xh = xh_ref[r, :]
        second = norm_back(g, xh, inv_ref[r, :], par_ref[1:2, :])
        second_ref[r, :] = second
        branch = second.astype(BF16)
        branch_ref[r, :] = branch
        gain_sum += col_sum(g * xh)
        shift_sum += col_sum(g)
        branch_sum += col_sum(branch.astype(F32))
    sums_ref[...] = jnp.zeros_like(sums_ref)
    sums_ref[1:2, :] = gain_sum
    sums_ref[7:8, :] = shift_sum
    sums_ref[6:7, :] = branch_sum


def second_back(g, xh, inv, par, behind):
    rows, width = xh.shape
    vmem = pl.BlockSpec(memory_space=pltpu.VMEM)
    return pl.pallas_call(
        norm_back_kernel,
        in_specs=[vmem] * 4 + [pl.BlockSpec(memory_space=pl.ANY)] * len(behind),
        out_specs=[vmem] * 3,
        out_shape=[
            jax.ShapeDtypeStruct((rows, width), F32),
            jax.ShapeDtypeStruct((rows, width), BF16),
            jax.ShapeDtypeStruct((8, width), F32),
        ],
        compiler_params=pltpu.CompilerParams(vmem_limit_bytes=VMEM_BYTES),
        cost_estimate=pl.CostEstimate(flops=int(3 * PEAK), bytes_accessed=0, transcendentals=0),
        name="second_back",
    )(g, xh, inv, par, *behind)


def feed_back_kernel(save, g_ref, xh2_ref, inv2_ref, xh1_ref, inv1_ref, slope_ref, wd_ref, wi_ref, wo_ref,
                     par_ref, *rest):
    if save:
        first_ref, dctx_ref, inner_ref, att_ref, sums_ref, bsum_ref, acc_ref, dact_ref = rest[1:]
        branch_ref = xh2_ref
    else:
        first_ref, dctx_ref, acc_ref, dact_ref, branch_ref, inner_ref, att_ref = rest
    rows, width = g_ref.shape
    step = pl.program_id(0)

    @pl.when(step == 0)
    def _():
        if save:
            acc_ref[...] = g_ref[...]
            sums_ref[...] = jnp.zeros_like(sums_ref)
        else:
            for r in chunks(rows):
                g = g_ref[r, :].astype(F32)
                second = norm_back(g, xh2_ref[r, :], inv2_ref[r, :], par_ref[1:2, :])
                acc_ref[r, :] = second
                branch_ref[r, :] = second.astype(BF16)

    dact_ref[...] = dot_nt(branch_ref[...], wd_ref[...])
    bin_sum = jnp.zeros((1, dact_ref.shape[1]), F32)
    for r in chunks(rows):
        inner = (dact_ref[r, :] * slope_ref[r, :].astype(F32)).astype(BF16)
        if save:
            inner_ref[0, r, :] = inner
        else:
            inner_ref[r, :] = inner
        if save:
            bin_sum += col_sum(inner.astype(F32))
    if save:
        bsum_ref[...] = bin_sum
    acc_ref[...] += dot_nt(inner_ref[0] if save else inner_ref[...], wi_ref[...])

    @pl.when(step == pl.num_programs(0) - 1)
    def _():
        gain_sum = shift_sum = att_sum = jnp.zeros((1, width), F32)
        for r in chunks(rows):
            g = acc_ref[r, :]
            xh = xh1_ref[r, :]
            first = norm_back(g, xh, inv1_ref[r, :], par_ref[0:1, :])
            first_ref[r, :] = first
            att = first.astype(BF16)
            att_ref[r, :] = att
            if save:
                gain_sum += col_sum(g * xh)
                shift_sum += col_sum(g)
                att_sum += col_sum(att.astype(F32))
        if save:
            sums_ref[0:1, :] = gain_sum
            sums_ref[5:6, :] = shift_sum
            sums_ref[4:5, :] = att_sum
        dctx_ref[...] = dot_nt(att_ref[...], wo_ref[...]).astype(BF16)


def feed_back(g, kept, w_out, w_in, w_down, par, save, behind=()):
    xh1, inv1, xh2, inv2, slope = kept
    rows, width = xh1.shape
    hidden = slope.shape[1]
    steps = hidden // TILE
    whole = lambda j: (0, 0)
    full = pl.BlockSpec((rows, width), whole)
    tile = pl.BlockSpec((rows, TILE), lambda j: (0, j))
    out_shape = [jax.ShapeDtypeStruct((rows, width), F32), jax.ShapeDtypeStruct((rows, width), BF16)]
    out_specs = [full, full]
    scratch = [pltpu.VMEM((rows, width), F32), pltpu.VMEM((rows, TILE), F32)]
    if save:
        out_shape += [
            jax.ShapeDtypeStruct((2, rows, hidden // 2), BF16),
            jax.ShapeDtypeStruct((rows, width), BF16),
            jax.ShapeDtypeStruct((8, width), F32),
            jax.ShapeDtypeStruct((1, hidden), F32),
        ]
        out_specs += [
            pl.BlockSpec((1, rows, TILE), lambda j: (j // (steps // 2), 0, j % (steps // 2))), full,
            pl.BlockSpec((8, width), whole),
            pl.BlockSpec((1, TILE), lambda j: (0, j)),
        ]
    else:
        scratch += [pltpu.VMEM((rows, width), BF16), pltpu.VMEM((rows, TILE), BF16), pltpu.VMEM((rows, width), BF16)]
    return pl.pallas_call(
        functools.partial(feed_back_kernel, save),
        grid=(steps,),
        in_specs=[
            full, full, pl.BlockSpec((rows, 1), whole), full, pl.BlockSpec((rows, 1), whole), tile,
            pl.BlockSpec((TILE, width), lambda j: (j, 0)),
            pl.BlockSpec((width, TILE), lambda j: (0, j)),
            pl.BlockSpec((width, width), whole),
            pl.BlockSpec((8, width), whole),
        ] + [pl.BlockSpec(memory_space=pl.ANY)] * len(behind),
        out_specs=out_specs,
        out_shape=out_shape,
        scratch_shapes=scratch,
        compiler_params=pltpu.CompilerParams(vmem_limit_bytes=VMEM_BYTES),
        cost_estimate=pl.CostEstimate(flops=int((15 if save else 12) * PEAK), bytes_accessed=0, transcendentals=0),
        name="feed_back_save" if save else "feed_back",
    )(g, xh2, inv2, xh1, inv1, slope, w_down, w_in, w_out, par, *behind)


def attend_back_kernel(save, qkv_ref, dctx_ref, lse_ref, idc_ref, idr_ref, wq_ref, wk_ref, wv_ref, first_ref, *rest):
    if save:
        dh_ref, dqkv_ref, sums_ref, mask_ref, acc_ref = rest[-5:]
    else:
        dh_ref, mask_ref, acc_ref = rest
    rows = first_ref.shape[0]
    step = pl.program_id(0)

    @pl.when(step == 0)
    def _():
        for r in chunks(rows):
            mask_ref[r, :] = jnp.where(idc_ref[r, :] == idr_ref[...], 0.0, -1e30)
        acc_ref[...] = first_ref[...]

    scale = HD ** (-0.5)
    q = qkv_ref[0] * jnp.asarray(scale, BF16)
    k = qkv_ref[1]
    v = qkv_ref[2]
    dctx = dctx_ref[...]
    keys_t = k.T
    dq_t = []
    dk = []
    dv = []
    for n in range(GROUP // HD):
        cols = slice(n * HD, (n + 1) * HD)
        lse = lse_ref[n:n + 1, :]
        st = dot_nt(k[:, cols], q[:, cols]) + mask_ref[...]
        pt = jnp.exp(st - lse)
        dpt = dot_nt(v[:, cols], dctx[:, cols])
        row = jnp.sum(pt * dpt, axis=0, keepdims=True)
        dst = (pt * (dpt - row)).astype(BF16)
        dv.append(dot_nn(pt.astype(BF16), dctx[:, cols]))
        dk.append(dot_nn(dst, q[:, cols]))
        dq_t.append(dot_nn(keys_t[cols, :], dst))
    dq = (jnp.concatenate(dq_t, axis=0).T * scale).astype(BF16)
    dk = jnp.concatenate(dk, axis=1).astype(BF16)
    dv = jnp.concatenate(dv, axis=1).astype(BF16)
    if save:
        for n, part in enumerate((dq, dk, dv)):
            offset = n * first_ref.shape[1] + step * GROUP
            dqkv_ref[:, pl.ds(pl.multiple_of(offset, GROUP), GROUP)] = part
        sums_ref[...] = jnp.zeros_like(sums_ref)
        sums_ref[2:3, :] = col_sum(dq.astype(F32))
        sums_ref[3:4, :] = col_sum(dv.astype(F32))
    acc_ref[...] += dot_nt(dq, wq_ref[...]) + dot_nt(dk, wk_ref[...]) + dot_nt(dv, wv_ref[...])

    @pl.when(step == pl.num_programs(0) - 1)
    def _():
        dh_ref[...] = acc_ref[...].astype(BF16)


def attend_back(qkv, dctx, lse, ids, w_qkv, first, save, behind=()):
    rows, width = first.shape
    steps = width // GROUP
    whole = lambda j: (0, 0)
    full = pl.BlockSpec((rows, width), whole)
    out_shape = [jax.ShapeDtypeStruct((rows, width), BF16)]
    out_specs = [full]
    if save:
        out_shape += [jax.ShapeDtypeStruct((rows, 3 * width), BF16), jax.ShapeDtypeStruct((8, width), F32)]
        out_specs += [
            pl.BlockSpec((rows, 3 * width), whole),
            pl.BlockSpec((8, GROUP), lambda j: (0, j)),
        ]
    return pl.pallas_call(
        functools.partial(attend_back_kernel, save),
        grid=(steps,),
        in_specs=[
            pl.BlockSpec((3, rows, GROUP), lambda j: (0, 0, j)),
            pl.BlockSpec((rows, GROUP), lambda j: (0, j)),
            pl.BlockSpec((8, rows), lambda j: (j, 0)),
            pl.BlockSpec((rows, 1), whole),
            pl.BlockSpec((1, rows), whole),
            pl.BlockSpec((width, GROUP), lambda j: (0, j)),
            pl.BlockSpec((width, GROUP), lambda j: (0, j + steps)),
            pl.BlockSpec((width, GROUP), lambda j: (0, j + 2 * steps)),
            full,
        ] + [pl.BlockSpec(memory_space=pl.ANY)] * len(behind),
        out_specs=out_specs,
        out_shape=out_shape,
        scratch_shapes=[pltpu.VMEM((rows, rows), F32), pltpu.VMEM((rows, width), F32)],
        compiler_params=pltpu.CompilerParams(vmem_limit_bytes=VMEM_BYTES),
        cost_estimate=pl.CostEstimate(flops=int(14 * PEAK), bytes_accessed=0, transcendentals=0),
        name="attend_back_save" if save else "attend_back",
    )(qkv, dctx, lse, ids[:, None], ids[None, :], w_qkv, w_qkv, w_qkv, first, *behind)


def lefts_kernel(core_ref, *refs):
    sources, outs = refs[:8], refs[9:]
    rows = sources[0].shape[0]
    for n, out in enumerate(outs):
        own, other = sources[2 * n], sources[2 * n + 1]
        out[:, :rows] = own[...].T
        out[:, rows:] = other[...].T


def lefts(core, pairs, act, act_other, behind):
    rows, width = pairs[0].shape
    steps = width // GROUP
    wide = act.shape[1] // steps
    tile = pl.BlockSpec((rows, GROUP), lambda i, c: (0, i))
    return pl.pallas_call(
        lefts_kernel,
        grid_spec=pltpu.PrefetchScalarGridSpec(
            num_scalar_prefetch=1,
            grid=(steps,),
            in_specs=[tile] * len(pairs) + [
                pl.BlockSpec((rows, wide), lambda i, c: (0, i)),
                pl.BlockSpec((rows, wide), lambda i, c: (0, i)),
                pl.BlockSpec(memory_space=pl.ANY),
            ],
            out_specs=[pl.BlockSpec((GROUP, 2 * rows), lambda i, c: (i, 0))] * (len(pairs) // 2)
            + [pl.BlockSpec((wide, 2 * rows), lambda i, c: (i, 0))],
        ),
        out_shape=[jax.ShapeDtypeStruct((width, 2 * rows), BF16)] * (len(pairs) // 2)
        + [jax.ShapeDtypeStruct((act.shape[1], 2 * rows), BF16)],
        compiler_params=pltpu.CompilerParams(vmem_limit_bytes=VMEM_BYTES),
        cost_estimate=pl.CostEstimate(flops=int(10 * PEAK), bytes_accessed=0, transcendentals=0),
        name="lefts",
    )(core, *pairs, act, act_other, behind)


def grad_kernel(count, core_ref, *refs):
    extra_ref, out_ref = refs[3 * count:-1], refs[-1]
    at = 0
    for n in range(count):
        left, own, other = refs[3 * n:3 * n + 3]
        rows, cols = other.shape
        mine = own[0] if len(own.shape) == 3 else own[...]
        total = dot_nn(left[:, :rows], mine) + dot_nn(left[:, rows:], other[...])
        out_ref[:, at:at + cols] = total.astype(BF16)
        at += cols
    if extra_ref:
        out_ref[:, at:] = extra_ref[0][...]


def grad(core, parts, extra, name):
    size = min(512, GROUP * (parts[0][0].shape[0] // 768))
    height = parts[0][0].shape[0]
    in_specs, args, cols = [], [], 0
    for left, own, other in parts:
        rows, part = other.shape
        in_specs.append(pl.BlockSpec((size, left.shape[1]), lambda i, c: (i, 0)))
        if own.ndim == 3:
            in_specs.append(pl.BlockSpec((1, rows, part), lambda i, c: (c[0], 0, 0)))
        elif own.shape[1] == part:
            in_specs.append(pl.BlockSpec((rows, part), lambda i, c: (0, 0)))
        else:
            in_specs.append(pl.BlockSpec((rows, part), lambda i, c: (0, c[0])))
        in_specs.append(pl.BlockSpec((rows, part), lambda i, c: (0, 0)))
        args += [left, own, other]
        cols += part
    if extra is not None:
        in_specs.append(pl.BlockSpec((size, extra.shape[1]), lambda i, c: (i, 0)))
        args.append(extra)
        cols += extra.shape[1]
    return pl.pallas_call(
        functools.partial(grad_kernel, len(parts)),
        grid_spec=pltpu.PrefetchScalarGridSpec(
            num_scalar_prefetch=1,
            grid=(height // size,),
            in_specs=in_specs,
            out_specs=pl.BlockSpec((size, cols), lambda i, c: (i, 0)),
        ),
        out_shape=jax.ShapeDtypeStruct((height, cols), BF16),
        compiler_params=pltpu.CompilerParams(vmem_limit_bytes=VMEM_BYTES),
        cost_estimate=pl.CostEstimate(flops=int(1 * PEAK), bytes_accessed=0, transcendentals=0),
        name=name,
    )(core, *args)


def turned(block, axis, by):
    count = lax.axis_size(axis)
    return lax.ppermute(block, axis, [(i, (i + by) % count) for i in range(count)])


def around(block, axis):
    return [block] + [turned(block, axis, d) for d in range(1, lax.axis_size(axis))]


def place_kernel(plan, outs, at_ref, *refs):
    sources, out_refs, sems = refs[:len(plan)], refs[-1 - outs:-1], refs[-1]
    copies = []
    for n, (ref, (which, pick, where)) in enumerate(zip(sources, plan)):
        copies.append(pltpu.make_async_copy(pick(ref), where(out_refs[which], at_ref), sems.at[n]))
    for copy in copies:
        copy.start()
    for copy in copies:
        copy.wait()


def place(at, groups, name, behind=()):
    plan = [(n, pick, where) for n, (_, pieces) in enumerate(groups) for _, pick, where in pieces]
    arrays = [piece[0] for _, pieces in groups for piece in pieces]
    anywhere = pl.BlockSpec(memory_space=pl.ANY)
    return pl.pallas_call(
        functools.partial(place_kernel, plan, len(groups)),
        in_specs=[pl.BlockSpec(memory_space=pltpu.SMEM)] + [anywhere] * (len(arrays) + len(behind)),
        out_specs=[pl.BlockSpec(memory_space=pltpu.VMEM)] * len(groups),
        out_shape=[jax.ShapeDtypeStruct(shape, BF16) for shape, _ in groups],
        scratch_shapes=[pltpu.SemaphoreType.DMA((len(arrays),))],
        compiler_params=pltpu.CompilerParams(vmem_limit_bytes=VMEM_SMALL),
        cost_estimate=pl.CostEstimate(flops=int(5 * PEAK), bytes_accessed=0, transcendentals=0),
        name=name,
    )(at, *arrays, *behind)


X, Y, Z, C = range(4)


def after(block, other):
    return block + (other[(slice(0, 1),) * other.ndim].reshape(()) * 0).astype(block.dtype)


def spread(block, axis):
    count = lax.axis_size(axis)
    return lax.all_to_all(jnp.broadcast_to(block[None], (count,) + block.shape), axis, 0, 0, tiled=True)


def pieces_x(block):
    return [
        (
            part,
            lambda ref, d=d: ref.at[d],
            lambda out, at, d=d, e=e: out.at[(at[X] + 4 - d) % 4, (at[C] + e) % 2],
        )
        for e, part in enumerate(around(block, "core"))
        for d in range(4)
    ]


def pieces_around(blocks):
    return [
        (
            part,
            lambda ref: ref,
            lambda out, at, d=d, e=e: out.at[(at[X] + 4 - d) % 4, (at[C] + e) % 2],
        )
        for d, block in enumerate(blocks)
        for e, part in enumerate(around(block, "core"))
    ]


def pieces_xy(block):
    part = block.shape[2]
    return [
        (
            swapped,
            lambda ref, d=d: ref.at[d],
            lambda out, at, d=d, e=e, g=g: out.at[
                (at[X] + 4 - d) % 4, (at[C] + e) % 2, :,
                pl.ds(pl.multiple_of((at[Y] + 4 - g) % 4 * part, 128), part),
            ],
        )
        for g, moved in enumerate(around(block, "y"))
        for e, swapped in enumerate(around(moved, "core"))
        for d in range(4)
    ]


def pieces_xz(block):
    return [
        (
            swapped,
            lambda ref, d=d: ref.at[d],
            lambda out, at, d=d, e=e, g=g: out.at[
                (at[X] + 4 - d) % 4, (at[C] + e) % 2, (at[Z] + g) % 2
            ],
        )
        for g, moved in enumerate(around(block, "zl"))
        for e, swapped in enumerate(around(moved, "core"))
        for d in range(4)
    ]


def other_core(block):
    return lax.ppermute(block, "core", SWAP)


def other_half(block, behind=None):
    there = 1 - lax.axis_index("core")
    if block.ndim == 3:
        send = lax.dynamic_index_in_dim(block, there, 0, keepdims=False)
    else:
        half = block.shape[1] // 2
        send = lax.dynamic_slice_in_dim(block, there * half, half, 1)
    return other_core(send if behind is None else after(send, behind))


WIDE = ("fsdp", "zl", "y")


def exchange_sum(block):
    return jnp.sum(lax.all_to_all(block, WIDE, 0, 0, tiled=True).astype(F32), axis=0)


def emit_kernel(in_ref, down_ref, g_in_ref, g_down_ref):
    rows = g_in_ref.shape[0]
    g_in_ref[...] = in_ref[...].astype(F32).reshape(rows, -1)
    pieces, _, rows, cols = down_ref.shape
    block = down_ref[...].astype(F32)
    for n in range(2 * pieces):
        at = (n % 2) * (cols // 2)
        g_down_ref[n * rows:(n + 1) * rows, :] = block[n // 2, 0, :, at:at + cols // 2]


def emit(early, width):
    pieces, cores, rows, _ = early.shape
    half, steps = width // 2, 2
    step = pieces // steps
    return pl.pallas_call(
        emit_kernel,
        grid=(steps, cores),
        in_specs=[
            pl.BlockSpec((step, 1, rows, 4 * half), lambda i, c: (i, c, 0, 0)),
            pl.BlockSpec((step, 1, rows, 4 * half), lambda i, c: (i, c, 0, 1)),
        ],
        out_specs=[
            pl.BlockSpec((step * rows, 4 * half), lambda i, c: (i, c)),
            pl.BlockSpec((2 * step * rows, 2 * half), lambda i, c: (c * steps + i, 0)),
        ],
        out_shape=[
            jax.ShapeDtypeStruct((pieces * rows, 8 * half), F32),
            jax.ShapeDtypeStruct((2 * cores * pieces * rows, 2 * half), F32),
        ],
        cost_estimate=pl.CostEstimate(flops=int(5 * PEAK), bytes_accessed=0, transcendentals=0),
        name="emit",
    )(early, early)


def joined(halves):
    return jnp.concatenate(halves, axis=-1).astype(F32)


def body(boundary, seq_ids, w_qkv, w_out, w_in, w_down, gains, biases, b_in):
    section = lax.axis_index("section")
    shard = lax.axis_index("fsdp")
    own = boundary[0, :, 0]
    micro, own_rows, width = own.shape
    shards = lax.axis_size("fsdp")
    rows = own_rows * shards
    hidden = b_in.shape[1] * shards
    piece = width // shards
    at = jnp.stack([lax.axis_index(name) for name in ("fsdp", "y", "zl", "core")]).astype(jnp.int32)

    small = jnp.concatenate([gains[0], biases[0], b_in[0].reshape(-1, piece)])
    small = jnp.pad(small.reshape(-1, width), ((0, 13), (0, 0)))
    padded = jnp.concatenate([own, jnp.zeros((shards - micro,) + own.shape[1:], BF16)])
    padded = jnp.concatenate([padded, jnp.broadcast_to(small[None], (shards,) + small.shape)], axis=1)

    half, part, cols = piece // 2, w_down.shape[1] // 4, w_in.shape[2] // 4
    own_in = lax.dynamic_slice(w_in[0], (at[C] * half, at[Y] * cols), (half, cols))
    own_down = lax.dynamic_slice_in_dim(w_down[0], (at[C] * 2 + at[Z]) * part, part, 0)
    own_out = lax.dynamic_slice_in_dim(w_out[0], at[C] * half, half, 0)
    own_qkv = lax.dynamic_slice_in_dim(w_qkv[0], at[C] * half, half, 0)
    in_blocks = around(jnp.concatenate([own_in, own_out]), "fsdp")
    down_blocks = around(after(own_down, in_blocks[1]), "fsdp")
    qkv_blocks = around(after(own_qkv, down_blocks[1]), "fsdp")
    padded = lax.all_to_all(padded, "fsdp", 0, 0, tiled=True)
    in_block = jnp.stack([block[:half] for block in in_blocks])
    out_block = jnp.stack([block[half:] for block in in_blocks])
    shape_x = (4, 2, half)
    (full_qkv,) = place(at, [(shape_x + (3 * width,), pieces_around(qkv_blocks))], "place_qkv")
    full_qkv = full_qkv.reshape(width, 3 * width)

    slot = padded[:, :own_rows].reshape(rows, width)
    small = padded[:, own_rows:own_rows + 3].reshape(shards, 12, piece)
    par = jnp.swapaxes(small[:, :8], 0, 1).reshape(8, width).astype(F32)
    bias_in = small[:, 8:].reshape(1, hidden).astype(F32)
    ids = lax.dynamic_index_in_dim(seq_ids[:, 0], jnp.minimum(shard, micro - 1), 0, keepdims=False)

    (ctx,) = attend(slot, full_qkv, par, ids, False)
    full_in, full_down, full_out = place(
        at,
        [
            (shape_x + (hidden,), pieces_xy(in_block)),
            ((4, 2, 2, part, width), pieces_xz(jnp.stack(down_blocks))),
            (shape_x + (width,), pieces_x(out_block)),
        ],
        "place_rest",
        [ctx],
    )
    full_in = full_in.reshape(width, hidden)
    full_down = full_down.reshape(hidden, width)
    full_out = full_out.reshape(width, width)
    middle = feed(slot, ctx, full_out, full_in, full_down, par, bias_in, False)[0]
    arrived = lax.ppermute(middle, "section", [(0, 1)])

    h = jnp.where(section == 0, slot, arrived)
    ctx, qkv, lse = attend(h, full_qkv, par, ids, True)
    core = at[C:]
    out, normed, xh1, inv1, xh2, inv2, slope, act, act_theirs = feed(
        h, ctx, full_out, full_in, full_down, par, bias_in, True, [core]
    )
    kept = (xh1, inv1, xh2, inv2, slope)

    cot = jnp.where(ids[:, None] >= 0, slot, jnp.zeros_like(slot))
    first, dctx = feed_back(cot, kept, full_out, full_in, full_down, par, False)
    (d_middle,) = attend_back(qkv, dctx, lse, ids, full_qkv, first, False)
    returned = lax.ppermute(d_middle, "section", [(1, 0)])

    pairs = [part for block in (h, normed, ctx) for part in (block, other_core(block))]
    h2, normed2, ctx2, act2 = lefts(core, pairs, act, other_core(act_theirs), d_middle)

    g = jnp.where(section == 0, returned, after(cot, h2))
    second, branch, sums2 = second_back(g, xh2, inv2, par, [h2, normed2, ctx2, act2])
    g_down = grad(core, [(act2, branch, other_core(branch))], None, "grad_down")
    s_down = exchange_sum(g_down.reshape(32, 48, width)).astype(BF16)
    first, dctx, inner, att, sums1, bin_sums = feed_back(
        second, (xh1, inv1, branch, inv2, slope), full_out, full_in, full_down, par, True, [g_down]
    )
    g_mid = grad(core, [(normed2, inner, other_half(inner))], None, "grad_mid")
    s_mid = exchange_sum(g_mid.reshape(32, 24, -1)).astype(BF16)
    d_h, dqkv, sums0 = attend_back(qkv, dctx, lse, ids, full_qkv, first, True, [g_mid, s_down])

    vec = (sums0 + sums1 + sums2).reshape(8, shards, piece)
    vec = jnp.concatenate([jnp.swapaxes(vec, 0, 1), bin_sums.reshape(shards, -1, piece)], axis=1)
    vec = jnp.pad(vec.reshape(shards, -1).astype(BF16), ((0, 0), (0, 768))).reshape(shards, 1, 24, 128)
    vec = jnp.broadcast_to(vec, (shards, 8, 24, 128)).reshape(768, 128)
    g_qkv = grad(
        core, [(h2, dqkv, other_half(dqkv)), (ctx2, att, other_half(att))], vec, "grad_qkv"
    ).reshape(32, 24, -1)
    half = g_qkv.shape[2] - 128
    s_qkv = exchange_sum(g_qkv)

    wide = 3 * width // 2
    early = [s_mid, after(s_down[:24], g_qkv), s_down[24:]]
    early = lax.all_gather(jnp.concatenate(early, axis=1), ("zl", "y", "core"))
    g_in, g_down = emit(early.reshape((8, 2) + early.shape[1:]), width)
    mine = spread(s_qkv[:, :half].astype(BF16), ("zl", "y"))
    other = lax.ppermute(mine, "core", SWAP)
    low = lax.axis_index("core") == 0
    pair = [jnp.where(low, mine, other), jnp.where(low, other, mine)]
    g_qkv = joined([part[..., :wide] for part in pair])
    g_out = joined([part[..., wide:] for part in pair])
    vec = s_qkv[:, half:]
    vec = (vec + lax.ppermute(vec, "core", SWAP)).reshape(-1)[:12 * piece].reshape(12, piece)

    ends = jnp.where(section == 0, d_h, out).reshape(shards, own_rows, width)
    home = jnp.zeros_like(ends)
    for d in range(shards):
        block = lax.dynamic_index_in_dim(ends, (shard + d) % shards, 0)
        block = turned(block, "fsdp", d) if d else block
        home = lax.dynamic_update_slice_in_dim(home, block, (shard + shards - d) % shards, 0)
    ends = home[:micro].astype(F32)
    return (
        ends[None, :, None],
        g_qkv.reshape(1, 192, -1),
        g_out.reshape(1, 192, -1),
        g_in[None],
        g_down[None],
        vec[None, :2],
        vec[None, 2:8],
        vec[None, 8:].reshape(1, -1),
    )


def solution(mesh):
    fine = Mesh(mesh.devices.reshape(2, 4, 2, 4, 2), ("section", "fsdp", "zl", "y", "core"))
    dp = ("zl", "y", "core")
    in_specs = (
        P("section", None, None, dp + ("fsdp",), None),
        P(None, None, dp),
        P("section", "fsdp", None),
        P("section", "fsdp", None),
        P("section", "fsdp", None),
        P("section", "fsdp", None),
        P("section", None, "fsdp"),
        P("section", None, "fsdp"),
        P("section", "fsdp"),
    )
    out_specs = (
        P("section", None, None, dp + ("fsdp",), None),
        P("section", "fsdp", None),
        P("section", "fsdp", None),
        P("section", "fsdp", None),
        P("section", "fsdp", None),
        P("section", None, "fsdp"),
        P("section", None, "fsdp"),
        P("section", "fsdp"),
    )
    return jax.shard_map(body, mesh=fine, in_specs=in_specs, out_specs=out_specs, check_vma=False)
```
